128 devices in a mesh: dp: 4 (over z), pipe: 8 (over y, x_lo), tensor: 4 (over x_hi, core).
Axes of the slice: x: 4 (x_hi: 2, x_lo: 2; x = x_hi * 2 + x_lo), y: 4, z: 4, core: 2. Of those that a mesh axis runs over, the one named last changes fastest.
Arguments:
- stream_a: bfloat16 [8, 32, 2048], P('dp', None, 'tensor'), may hold values from -6 to 6
- stream_b: bfloat16 [8, 32, 2048], P('dp', None, 'tensor'), may hold values from -6 to 6
- target_a: bfloat16 [8, 32, 2048], P('dp', None, 'tensor'), may hold values from -0.75 to 0.75
- target_b: bfloat16 [8, 32, 2048], P('dp', None, 'tensor'), may hold values from -0.75 to 0.75
- up_weight: bfloat16 [8, 2048, 4096], P('pipe', None, 'tensor'), may hold values from -0.125 to 0.125
- down_weight: bfloat16 [8, 4096, 2048], P('pipe', 'tensor'), may hold values from -0.09375 to 0.09375
Outputs:
- up_grad: float32 [8, 2048, 4096], P('pipe', 'dp', 'tensor')
- down_grad: float32 [8, 4096, 2048], P('pipe', 'tensor', 'dp')
The draws below stay inside these ranges and needn't reach their ends.
All inputs are finite; a program needn't handle non-finite values.
Results may differ from the reference program's by a relative error of at most 0.03.
Values may be sent and summed in bfloat16 or wider, within the bound.
No kernel may reach another device: no remote copies, remote signals or barrier semaphores. Data moves between devices by JAX's collectives and lax.ppermute only.
A program may use at most 64 MiB of HBM per device.

```python
import jax
import jax.numpy as jnp
from jax import lax

MODEL_WIDTH = 2048
FF = 4096
SEQ = 32
MICRO = 2
LAYERS = 8
BATCH = 8
N_DP = 4


def steps_of(stream_key, shape, pieces, least, top_value):
    gain = 1.0
    for position, shards_of in pieces:
        heights = jax.random.uniform(jax.random.fold_in(jax.random.fold_in(stream_key, 6), position), (shards_of,), jnp.float32, least / len(pieces), top_value / len(pieces))
        gain = gain * jnp.repeat(jnp.exp(heights), shape[position] // shards_of).reshape((-1,) + (1,) * (len(shape) - 1 - position))
    return gain


def centred(own_key, shape, width, limit, shards=(), dtype=jnp.bfloat16):
    result = width * jax.random.normal(own_key, shape, jnp.float32)
    if shards:
        result = result * steps_of(own_key, shape, shards, -0.22, 0.18)
    return jnp.clip(result, -limit, limit).astype(dtype)


def setup_inputs(seed: int = 0) -> dict:
    arg_keys = jax.random.split(jax.random.key(seed), 7)
    stream_a = centred(arg_keys[0], (BATCH, SEQ, MODEL_WIDTH), 1.0, 6.0, ((0, 4), (2, 4)))
    stream_b = centred(arg_keys[1], (BATCH, SEQ, MODEL_WIDTH), 1.0, 6.0, ((0, 4), (2, 4)))
    target_a = centred(arg_keys[2], (BATCH, SEQ, MODEL_WIDTH), 0.05, 0.75, ((0, 4), (2, 4)))
    target_b = centred(arg_keys[3], (BATCH, SEQ, MODEL_WIDTH), 0.05, 0.75, ((0, 4), (2, 4)))
    up_weight = centred(arg_keys[4], (LAYERS, MODEL_WIDTH, FF), MODEL_WIDTH ** -0.5, 0.125, ((0, 8), (2, 4)))
    down_weight = centred(arg_keys[5], (LAYERS, FF, MODEL_WIDTH), FF ** -0.5, 0.09375, ((0, 8), (1, 4)))
    return {"stream_a": stream_a, "stream_b": stream_b, "target_a": target_a, "target_b": target_b, "up_weight": up_weight, "down_weight": down_weight}


epsilon = 1e-06
contract_last = (((1,), (1,)), ((), ()))
contract_first = (((0,), (0,)), ((), ()))

def smooth(value):
    return jax.nn.gelu(value, approximate=True)

def layer_forward(token_rows, up, down):
    wide = token_rows.astype(jnp.float32)
    norm_scale = lax.rsqrt(lax.optimization_barrier(jnp.sum(wide * wide, axis=1, keepdims=True)) / MODEL_WIDTH + epsilon)
    normed = (wide * norm_scale).astype(jnp.bfloat16)
    hidden = jnp.dot(normed, up, preferred_element_type=jnp.float32)
    active = smooth(hidden).astype(jnp.bfloat16)
    output = (wide + jnp.dot(active, down, preferred_element_type=jnp.float32)).astype(jnp.bfloat16)
    return (output, (token_rows, norm_scale, normed, hidden, active))

def layer_backward(gradient_rows, saved, up, down):
    token_rows, norm_scale, normed, hidden, active = saved
    back = lax.dot_general(gradient_rows, down, contract_last, preferred_element_type=jnp.float32)
    _, pull = jax.vjp(smooth, hidden)
    delta = pull(back)[0].astype(jnp.bfloat16)
    forward_send = lax.dot_general(delta, up, contract_last, preferred_element_type=jnp.float32)
    normalized_input = token_rows.astype(jnp.float32) * norm_scale
    inner_product = lax.optimization_barrier(jnp.sum(forward_send * normalized_input, axis=1, keepdims=True))
    relay_result = (gradient_rows.astype(jnp.float32) + norm_scale * (forward_send - normalized_input * inner_product / MODEL_WIDTH)).astype(jnp.bfloat16)
    return (relay_result, delta)

def reference(stream_a, stream_b, target_a, target_b, up_weight, down_weight):
    up_total = jnp.zeros((LAYERS, MODEL_WIDTH, FF), jnp.float32)
    down_total = jnp.zeros((LAYERS, FF, MODEL_WIDTH), jnp.float32)
    for replica in range(N_DP):
        collected = [[] for layer in range(LAYERS)]
        for source, target in ((stream_a, target_a), (stream_b, target_b)):
            token_rows = source[replica * MICRO:(replica + 1) * MICRO].reshape(MICRO * SEQ, MODEL_WIDTH)
            saved = []
            for layer in range(LAYERS):
                token_rows, items = layer_forward(token_rows, up_weight[layer], down_weight[layer])
                saved.append(items)
            gradient_rows = target[replica * MICRO:(replica + 1) * MICRO].reshape(MICRO * SEQ, MODEL_WIDTH)
            for layer in range(LAYERS - 1, -1, -1):
                incoming = gradient_rows
                gradient_rows, delta = layer_backward(gradient_rows, saved[layer], up_weight[layer], down_weight[layer])
                collected[layer].append((saved[layer][2], delta, saved[layer][4], incoming))
        for layer in range(LAYERS):
            normed = jnp.concatenate([item[0] for item in collected[layer]], axis=0)
            delta = jnp.concatenate([item[1] for item in collected[layer]], axis=0)
            active = jnp.concatenate([item[2] for item in collected[layer]], axis=0)
            incoming = jnp.concatenate([item[3] for item in collected[layer]], axis=0)
            term_up = lax.dot_general(normed, delta, contract_first, preferred_element_type=jnp.float32).astype(jnp.bfloat16)
            term_down = lax.dot_general(active, incoming, contract_first, preferred_element_type=jnp.float32).astype(jnp.bfloat16)
            up_total = up_total.at[layer].add(term_up.astype(jnp.float32))
            down_total = down_total.at[layer].add(term_down.astype(jnp.float32))
    return (up_total, down_total)
```

```python
import jax
import jax.numpy as jnp
from jax import lax
from jax.sharding import PartitionSpec as P

MODEL_WIDTH = 2048

epsilon = 1e-06
contract_last = (((1,), (1,)), ((), ()))
contract_first = (((0,), (0,)), ((), ()))
grid = ("pipe", "tensor")


def from_core(value):
    return lax.ppermute(value, "tensor", [(i, i ^ 1) for i in range(4)])


def neighbour(rank, odd, ranks):
    if odd:
        return (((rank + 1) ^ 1) - 1) % ranks
    return rank ^ 1


def from_rank(value, odd, flip):
    ranks = lax.axis_size("pipe")
    tensors = lax.axis_size("tensor")
    pairs = [
        (p * tensors + t, neighbour(p, odd, ranks) * tensors + (t ^ flip))
        for p in range(ranks)
        for t in range(tensors)
    ]
    return lax.ppermute(value, grid, pairs)


def from_replica(value, by):
    groups = lax.axis_size("dp")
    return lax.ppermute(value, "dp", [(i, (i + by) % groups) for i in range(groups)])


def gelu_pair(value):
    root = jnp.float32(0.7978845608028654)
    square = value * value
    inner = root * (value + 0.044715 * square * value)
    bend = jnp.tanh(inner)
    half = 0.5 * (1.0 + bend)
    slope = half + 0.5 * value * (1.0 - bend * bend) * root * (1.0 + 3 * 0.044715 * square)
    return value * half, slope


def whole_rows(piece, core):
    across = from_rank(piece, False, 2)
    upper = lax.axis_index("tensor") // 2
    first = jnp.where(upper == 0, piece, across)
    second = jnp.where(upper == 0, across, piece)
    mine = jnp.concatenate([first, second], axis=1)
    theirs = from_core(mine)
    low = jnp.where(core == 0, mine, theirs)
    high = jnp.where(core == 0, theirs, mine)
    share = piece.shape[1]
    full = jnp.concatenate(
        [low[:, :share], high[:, :share], low[:, share:], high[:, share:]], axis=1
    )
    rows = full.shape[0] // 2
    swapped = jnp.concatenate([full[rows:], full[:rows]], axis=0)
    return jnp.where(core == 0, full, swapped)


def relay(part, odd):
    rows = part.shape[0] // 2
    theirs = from_core(part[rows:].astype(jnp.bfloat16))
    chip = (part[:rows] + theirs.astype(jnp.float32)).astype(jnp.bfloat16)
    straight = from_rank(chip, odd, 0)
    across = from_rank(chip, odd, 2)
    mine = (straight.astype(jnp.float32) + across.astype(jnp.float32)).astype(jnp.bfloat16)
    return jnp.concatenate([mine, from_core(mine)], axis=0)


def local(stream_a, stream_b, target_a, target_b, up_weight, down_weight):
    ranks = lax.axis_size("pipe")
    place = lax.axis_index("pipe")
    core = lax.axis_index("tensor") % 2
    groups = lax.axis_size("dp")
    member = lax.axis_index("dp")
    up = up_weight[0]
    down = down_weight[0]
    share = stream_a.shape[2]
    flat = lambda value: value.reshape(-1, share)
    rows = [whole_rows(flat(value), core) for value in (stream_a, stream_b)]
    grads = [whole_rows(flat(value), core) for value in (target_a, target_b)]
    saved = [None, None]
    for step in range(ranks):
        here = place == step
        for slot in range(2):
            wide = rows[slot].astype(jnp.float32)
            scale = lax.rsqrt(jnp.mean(wide * wide, axis=1, keepdims=True) + epsilon)
            normed = (wide * scale).astype(jnp.bfloat16)
            hidden = jnp.dot(normed, up, preferred_element_type=jnp.float32)
            active, slope = gelu_pair(hidden)
            active = active.astype(jnp.bfloat16)
            items = (rows[slot], scale, normed, active, slope)
            if step == 0:
                saved[slot] = items
            else:
                saved[slot] = tuple(
                    jnp.where(here, item, kept) for item, kept in zip(items, saved[slot])
                )
            if step < ranks - 1:
                part = jnp.dot(active, down, preferred_element_type=jnp.float32) + 0.25 * wide
                rows[slot] = relay(part, step % 2 == 1)

    def every(values, by):
        return from_replica(values, by) if by else values

    def cut(value, by):
        return lax.dynamic_slice_in_dim(value, ((member + by) % groups) * share, share, 1)

    normed = jnp.concatenate([saved[0][2], saved[1][2]], axis=0)
    active = jnp.concatenate([saved[0][3], saved[1][3]], axis=0)
    all_normed = jnp.concatenate([every(cut(normed, by), by) for by in range(groups)], axis=0)
    all_active = jnp.concatenate([every(active, by) for by in range(groups)], axis=0)

    kept = [None, None]
    for step in range(ranks):
        here = place == ranks - 1 - step
        for slot in range(2):
            held, scale, normed, active, slope = saved[slot]
            back = lax.dot_general(
                grads[slot], down, contract_last, preferred_element_type=jnp.float32
            )
            delta = (back * slope).astype(jnp.bfloat16)
            items = (grads[slot], delta)
            if step == 0:
                kept[slot] = items
            else:
                kept[slot] = tuple(
                    jnp.where(here, item, old) for item, old in zip(items, kept[slot])
                )
            if step < ranks - 1:
                push = lax.dot_general(
                    delta, up, contract_last, preferred_element_type=jnp.float32
                )
                unit = held.astype(jnp.float32) * scale
                inner = jnp.sum(push * unit, axis=1, keepdims=True) / MODEL_WIDTH
                part = 0.25 * grads[slot].astype(jnp.float32) + scale * (push - unit * inner)
                grads[slot] = relay(part, step % 2 == 1)
    grad = jnp.concatenate([kept[0][0], kept[1][0]], axis=0)
    delta = jnp.concatenate([kept[0][1], kept[1][1]], axis=0)
    all_grad = jnp.concatenate([every(cut(grad, by), by) for by in range(groups)], axis=0)
    all_delta = jnp.concatenate([every(delta, by) for by in range(groups)], axis=0)
    up_sum = lax.dot_general(
        all_normed, all_delta, contract_first, preferred_element_type=jnp.float32
    )
    down_sum = lax.dot_general(
        all_active, all_grad, contract_first, preferred_element_type=jnp.float32
    )
    return (up_sum[None], down_sum[None])


def solution(mesh):
    return jax.shard_map(
        local,
        mesh=mesh,
        in_specs=(
            P("dp", None, "tensor"),
            P("dp", None, "tensor"),
            P("dp", None, "tensor"),
            P("dp", None, "tensor"),
            P("pipe", None, "tensor"),
            P("pipe", "tensor", None),
        ),
        out_specs=(P("pipe", "dp", "tensor"), P("pipe", "tensor", "dp")),
        check_vma=False,
    )
```

```python
import jax
import jax.numpy as jnp
from jax import lax
from jax.sharding import PartitionSpec as P

MODEL_WIDTH = 2048

epsilon = 1e-06
contract_last = (((1,), (1,)), ((), ()))
contract_first = (((0,), (0,)), ((), ()))
grid = ("pipe", "tensor")


def from_core(value):
    return lax.ppermute(value, "tensor", [(i, i ^ 1) for i in range(4)])


def from_rank(value, by, flip):
    ranks = lax.axis_size("pipe")
    tensors = lax.axis_size("tensor")
    pairs = [
        (p * tensors + t, (p + by) % ranks * tensors + (t ^ flip))
        for p in range(ranks)
        for t in range(tensors)
    ]
    return lax.ppermute(value, grid, pairs)


def from_twin(value):
    ranks = lax.axis_size("pipe")
    tensors = lax.axis_size("tensor")
    pairs = [
        (p * tensors + t, (p ^ 1) * tensors + (t ^ 2))
        for p in range(ranks)
        for t in range(tensors)
    ]
    return lax.ppermute(value, grid, pairs)


def from_replica(value, by):
    groups = lax.axis_size("dp")
    return lax.ppermute(value, "dp", [(i, (i + by) % groups) for i in range(groups)])


def gelu_pair(value):
    root = jnp.float32(0.7978845608028654)
    square = value * value
    inner = root * (value + 0.044715 * square * value)
    bend = jnp.tanh(inner)
    half = 0.5 * (1.0 + bend)
    slope = half + 0.5 * value * (1.0 - bend * bend) * root * (1.0 + 3 * 0.044715 * square)
    return value * half, slope


def whole_rows(piece, core, chunks):
    across = from_twin(piece)
    upper = lax.axis_index("tensor") // 2
    first = jnp.where(upper == 0, piece, across)
    second = jnp.where(upper == 0, across, piece)
    mine = jnp.concatenate([first, second], axis=1)
    theirs = from_core(mine)
    low = jnp.where(core == 0, mine, theirs)
    high = jnp.where(core == 0, theirs, mine)
    share = piece.shape[1]
    full = jnp.concatenate(
        [low[:, :share], high[:, :share], low[:, share:], high[:, share:]], axis=1
    )
    halves = full.reshape(chunks, 2, -1, full.shape[1])
    own = jnp.where(core == 0, halves[:, 0], halves[:, 1])
    rest = jnp.where(core == 0, halves[:, 1], halves[:, 0])
    return jnp.concatenate([own, rest], axis=1)


def relay(part, by):
    rows = part.shape[0] // 2
    theirs = from_core(part[rows:].astype(jnp.bfloat16))
    chip = (part[:rows] + theirs.astype(jnp.float32)).astype(jnp.bfloat16)
    straight = from_rank(chip, by, 0)
    across = from_rank(chip, by, 2)
    mine = (straight.astype(jnp.float32) + across.astype(jnp.float32)).astype(jnp.bfloat16)
    return jnp.concatenate([mine, from_core(mine)], axis=0)


def put(stack, item, index):
    return lax.dynamic_update_index_in_dim(stack, item, index, 0)


def take(stack, index):
    return lax.dynamic_index_in_dim(stack, index, 0, keepdims=False)


def local(stream_a, stream_b, target_a, target_b, up_weight, down_weight):
    ranks = lax.axis_size("pipe")
    place = lax.axis_index("pipe")
    core = lax.axis_index("tensor") % 2
    groups = lax.axis_size("dp")
    member = lax.axis_index("dp")
    up = up_weight[0]
    down = down_weight[0]
    share = stream_a.shape[2]
    tokens = stream_a.shape[1]
    hid = up.shape[1]
    chunks = 2 * stream_a.shape[0]
    source = jnp.concatenate([stream_a, stream_b], axis=0).reshape(-1, share)
    target = jnp.concatenate([target_a, target_b], axis=0).reshape(-1, share)
    source = whole_rows(source, core, chunks)
    target = whole_rows(target, core, chunks)
    stash = (
        jnp.zeros((chunks + 1, tokens, 1), jnp.float32),
        jnp.zeros((chunks + 1, tokens, MODEL_WIDTH), jnp.bfloat16),
        jnp.zeros((chunks + 1, tokens, hid), jnp.bfloat16),
        jnp.zeros((chunks + 1, tokens, hid), jnp.float32),
    )
    kept = (
        jnp.zeros((chunks + 1, tokens, MODEL_WIDTH), jnp.bfloat16),
        jnp.zeros((chunks + 1, tokens, hid), jnp.bfloat16),
    )
    steps = ranks + chunks - 1
    rows = None
    grad = None
    gathered = None

    def every(value, by):
        return from_replica(value, by) if by else value

    def cut(value, by):
        return lax.dynamic_slice_in_dim(value, ((member + by) % groups) * share, share, 1)

    def spread(wide, narrow):
        wide = wide[:chunks].reshape(-1, MODEL_WIDTH)
        narrow = narrow[:chunks].reshape(-1, hid)
        return (
            jnp.concatenate([every(cut(wide, by), by) for by in range(groups)], axis=0),
            jnp.concatenate([every(narrow, by) for by in range(groups)], axis=0),
        )

    for step in range(steps + ranks):
        if step < steps:
            if step == 0:
                rows = source[0]
            elif step < chunks:
                rows = jnp.where(place == 0, source[step], rows)
            slot = jnp.clip(step - place, 0, chunks)
            wide = rows.astype(jnp.float32)
            scale = lax.rsqrt(jnp.mean(wide * wide, axis=1, keepdims=True) + epsilon)
            normed = (wide * scale).astype(jnp.bfloat16)
            hidden = jnp.dot(normed, up, preferred_element_type=jnp.float32)
            active, slope = gelu_pair(hidden)
            active = active.astype(jnp.bfloat16)
            stash = tuple(
                put(stack, item, slot)
                for stack, item in zip(stash, (scale, normed, active, slope))
            )
            if step < steps - 1:
                part = jnp.dot(active, down, preferred_element_type=jnp.float32) + 0.25 * wide
                rows = relay(part, 1)
        if step == steps:
            gathered = spread(stash[1], stash[2])
        if step >= ranks:
            turn = step - ranks
            if turn == 0:
                grad = target[0]
            elif turn < chunks:
                grad = jnp.where(place == ranks - 1, target[turn], grad)
            slot = jnp.clip(turn - (ranks - 1 - place), 0, chunks)
            scale, normed, active, slope = (take(stack, slot) for stack in stash)
            back = lax.dot_general(grad, down, contract_last, preferred_element_type=jnp.float32)
            delta = (back * slope).astype(jnp.bfloat16)
            kept = tuple(put(stack, item, slot) for stack, item in zip(kept, (grad, delta)))
            if turn < steps - 1:
                push = lax.dot_general(
                    delta, up, contract_last, preferred_element_type=jnp.float32
                )
                unit = normed.astype(jnp.float32)
                inner = jnp.sum(push * unit, axis=1, keepdims=True) / MODEL_WIDTH
                part = 0.25 * grad.astype(jnp.float32) + scale * (push - unit * inner)
                grad = relay(part, -1)
    all_normed, all_active = gathered
    all_grad, all_delta = spread(*kept)
    up_sum = lax.dot_general(
        all_normed, all_delta, contract_first, preferred_element_type=jnp.float32
    )
    down_sum = lax.dot_general(
        all_active, all_grad, contract_first, preferred_element_type=jnp.float32
    )
    return (up_sum[None], down_sum[None])


def solution(mesh):
    return jax.shard_map(
        local,
        mesh=mesh,
        in_specs=(
            P("dp", None, "tensor"),
            P("dp", None, "tensor"),
            P("dp", None, "tensor"),
            P("dp", None, "tensor"),
            P("pipe", None, "tensor"),
            P("pipe", "tensor", None),
        ),
        out_specs=(P("pipe", "dp", "tensor"), P("pipe", "tensor", "dp")),
        check_vma=False,
    )
```

```python
import jax
import jax.numpy as jnp
from jax import lax
from jax.experimental import pallas as pl
from jax.experimental.pallas import tpu as pltpu
from jax.sharding import PartitionSpec as P

MODEL_WIDTH = 2048

CHUNKS = 4

epsilon = 1e-06
contract_last = (((1,), (1,)), ((), ()))
contract_first = (((0,), (0,)), ((), ()))
grid = ("pipe", "tensor")


def from_core(value):
    return lax.ppermute(value, "tensor", [(i, i ^ 1) for i in range(4)])


def to_rank(value, by):
    ranks = lax.axis_size("pipe")
    tensors = lax.axis_size("tensor")
    pairs = [
        (p * tensors + t, (p + by) % ranks * tensors + t % 2 * 2 + t // 2)
        for p in range(ranks)
        for t in range(tensors)
    ]
    return lax.ppermute(value, grid, pairs)


def from_twin(value):
    ranks = lax.axis_size("pipe")
    tensors = lax.axis_size("tensor")
    pairs = [
        (p * tensors + t, (p ^ 1) * tensors + (t ^ 2))
        for p in range(ranks)
        for t in range(tensors)
    ]
    return lax.ppermute(value, grid, pairs)


def from_replica(value, by):
    groups = lax.axis_size("dp")
    return lax.ppermute(value, "dp", [(i, (i + by) % groups) for i in range(groups)])


def gelu_pair(value):
    root = jnp.float32(0.7978845608028654)
    square = value * value
    inner = root * (value + 0.044715 * square * value)
    bend = jnp.tanh(inner)
    half = 0.5 * (1.0 + bend)
    slope = half + 0.5 * value * (1.0 - bend * bend) * root * (1.0 + 3 * 0.044715 * square)
    return value * half, slope


def whole_rows(piece, core):
    across = from_twin(piece)
    upper = lax.axis_index("tensor") // 2
    first = jnp.where(upper == 0, piece, across)
    second = jnp.where(upper == 0, across, piece)
    mine = jnp.concatenate([first, second], axis=1)
    theirs = from_core(mine)
    low = jnp.where(core == 0, mine, theirs)
    high = jnp.where(core == 0, theirs, mine)
    share = piece.shape[1]
    return jnp.concatenate(
        [low[:, :share], high[:, :share], low[:, share:], high[:, share:]], axis=1
    )


def send(part, by):
    theirs = from_core(part.astype(jnp.bfloat16))
    return to_rank((part + theirs.astype(jnp.float32)).astype(jnp.bfloat16), by)


def settle(come):
    return (come.astype(jnp.float32) + from_core(come).astype(jnp.float32)).astype(jnp.bfloat16)


def turn_block(from_ref, token_ref, to_ref):
    block = from_ref.shape[0]
    row = lax.broadcasted_iota(jnp.int32, (block, block), 0)
    column = lax.broadcasted_iota(jnp.int32, (block, block), 1)
    unit = jnp.where(row == column, 1.0, 0.0).astype(jnp.bfloat16)
    for first in range(0, from_ref.shape[1], block):
        to_ref[first : first + block, :] = lax.dot_general(
            unit,
            from_ref[:, first : first + block],
            contract_last,
            preferred_element_type=jnp.float32,
        ).astype(jnp.bfloat16)


def turned(weight, token, block):
    rows, columns = weight.shape
    return pl.pallas_call(
        turn_block,
        out_shape=jax.ShapeDtypeStruct((columns, rows), weight.dtype),
        grid=(rows // block,),
        in_specs=[
            pl.BlockSpec((block, columns), lambda i: (i, 0)),
            pl.BlockSpec(memory_space=pl.ANY),
        ],
        out_specs=pl.BlockSpec((columns, block), lambda i: (0, i)),
        compiler_params=pltpu.CompilerParams(vmem_limit_bytes=6 * 2**20),
        cost_estimate=pl.CostEstimate(
            flops=2 * rows * columns * block, bytes_accessed=4 * rows * columns, transcendentals=0
        ),
    )(weight, token)


def put(stack, item, index):
    return lax.dynamic_update_index_in_dim(stack, item, index, 0)


def take(stack, index):
    return lax.dynamic_index_in_dim(stack, index, 0, keepdims=False)


def terms(first, second, share):
    up_term = lax.dot_general(
        first[:, :share], second[:, share:], contract_first, preferred_element_type=jnp.float32
    )
    down_term = lax.dot_general(
        first[:, share:], second[:, :share], contract_first, preferred_element_type=jnp.float32
    )
    return up_term, down_term


def local(stream_a, stream_b, target_a, target_b, up_weight, down_weight):
    ranks = lax.axis_size("pipe")
    place = lax.axis_index("pipe")
    core = lax.axis_index("tensor") % 2
    groups = lax.axis_size("dp")
    member = lax.axis_index("dp")
    up = up_weight[0]
    down = down_weight[0]
    share = stream_a.shape[2]
    hid = up.shape[1]
    source = jnp.concatenate([stream_a, stream_b], axis=0).reshape(-1, share)
    source = whole_rows(source, core).reshape(CHUNKS, -1, MODEL_WIDTH)
    tokens = source.shape[1]
    stash = (
        jnp.zeros((CHUNKS + 1, tokens, 1), jnp.float32),
        jnp.zeros((CHUNKS + 1, tokens, MODEL_WIDTH), jnp.bfloat16),
        jnp.zeros((CHUNKS + 1, tokens, hid), jnp.bfloat16),
        jnp.zeros((CHUNKS + 1, tokens, hid), jnp.float32),
    )
    kept = (
        jnp.zeros((CHUNKS + 1, tokens, MODEL_WIDTH), jnp.bfloat16),
        jnp.zeros((CHUNKS + 1, tokens, hid), jnp.bfloat16),
    )
    steps = ranks + CHUNKS - 1
    rows = None
    grad = None
    ahead_parts = None
    behind_parts = []

    def cut(value, by):
        return lax.dynamic_slice_in_dim(value, ((member + by) % groups) * share, share, 1)

    def spread(wide, narrow):
        wide = wide.reshape(-1, MODEL_WIDTH)
        narrow = narrow.reshape(-1, hid)
        parts = []
        for by in range(groups):
            both = jnp.concatenate([cut(wide, by), narrow], axis=1)
            parts.append(from_replica(both, by) if by else both)
        return parts

    for step in range(steps + ranks - 1):
        turn = step - (ranks - 1)
        if step < steps:
            if step == 0:
                now = source[0]
            else:
                if step == 3:
                    rows, down_turned = lax.optimization_barrier((rows, down_turned))
                if step == 4:
                    rows, up_turned = lax.optimization_barrier((rows, up_turned))
                now = settle(rows)
                if step < CHUNKS:
                    now = jnp.where(place == 0, source[step], now)
            slot = jnp.clip(step - place, 0, CHUNKS)
            wide = now.astype(jnp.float32)
            scale = lax.rsqrt(jnp.mean(wide * wide, axis=1, keepdims=True) + epsilon)
            normed = (wide * scale).astype(jnp.bfloat16)
            if step == 1:
                target = jnp.concatenate([target_a, target_b], axis=0).reshape(-1, share)
                target, normed = lax.optimization_barrier((target, normed))
                target = whole_rows(target, core).reshape(CHUNKS, -1, MODEL_WIDTH)
            if step == 2:
                down_turned = turned(down, now, 256)
            if step == 3:
                up_turned = turned(up, now, 256)
            hidden = jnp.dot(normed, up, preferred_element_type=jnp.float32)
            active, slope = gelu_pair(hidden)
            active = active.astype(jnp.bfloat16)
            items = (scale, normed, active, slope)
            stash = tuple(put(stack, item, slot) for stack, item in zip(stash, items))
            if step < steps - 1:
                part = jnp.dot(active, down, preferred_element_type=jnp.float32) + 0.25 * wide
                rows = send(part, 1)
        if step == steps:
            all_normed = lax.all_gather(stash[1][:CHUNKS], "dp")
            all_active = lax.all_gather(stash[2][:CHUNKS], "dp")
        if turn >= 0:
            if turn == 0:
                now = target[0]
            else:
                if step == steps + 3:
                    grad, all_normed, all_active = lax.optimization_barrier(
                        (grad, all_normed, all_active)
                    )
                now = settle(grad)
                if turn < CHUNKS:
                    now = jnp.where(place == ranks - 1, target[turn], now)
            slot = jnp.clip(turn - (ranks - 1 - place), 0, CHUNKS)
            back = jnp.dot(now, down_turned, preferred_element_type=jnp.float32)
            scale, normed, active, slope = (take(stack, slot) for stack in stash)
            delta = (back * slope).astype(jnp.bfloat16)
            kept = tuple(put(stack, item, slot) for stack, item in zip(kept, (now, delta)))
            if turn < steps - 1:
                push = jnp.dot(delta, up_turned, preferred_element_type=jnp.float32)
                unit = normed.astype(jnp.float32)
                inner = jnp.sum(push * unit, axis=1, keepdims=True) / MODEL_WIDTH
                part = 0.25 * now.astype(jnp.float32) + scale * (push - unit * inner)
                grad = send(part, -1)
    last_parts = spread(kept[0][:CHUNKS], kept[1][:CHUNKS])
    first = []
    for by in range(groups):
        origin = (member - by) % groups
        wide = take(all_normed, origin).reshape(-1, MODEL_WIDTH)
        narrow = take(all_active, origin).reshape(-1, hid)
        first.append(jnp.concatenate([cut(wide, 0), narrow], axis=1))
    first = jnp.concatenate(first, axis=0)
    second = jnp.concatenate(last_parts, axis=0)
    up_sum, down_sum = terms(first, second, share)
    return (up_sum[None], down_sum[None])


def solution(mesh):
    return jax.shard_map(
        local,
        mesh=mesh,
        in_specs=(
            P("dp", None, "tensor"),
            P("dp", None, "tensor"),
            P("dp", None, "tensor"),
            P("dp", None, "tensor"),
            P("pipe", None, "tensor"),
            P("pipe", "tensor", None),
        ),
        out_specs=(P("pipe", "dp", "tensor"), P("pipe", "tensor", "dp")),
        check_vma=False,
    )
```

```python
import jax
import jax.numpy as jnp
from jax import lax
from jax.experimental import pallas as pl
from jax.experimental.pallas import tpu as pltpu
from jax.sharding import PartitionSpec as P

MODEL_WIDTH = 2048

CHUNKS = 4

epsilon = 1e-06
contract_last = (((1,), (1,)), ((), ()))
contract_first = (((0,), (0,)), ((), ()))
grid = ("pipe", "tensor")


def from_core(value):
    return lax.ppermute(value, "tensor", [(i, i ^ 1) for i in range(4)])


def to_rank(value, by):
    ranks = lax.axis_size("pipe")
    tensors = lax.axis_size("tensor")
    pairs = [
        (p * tensors + t, (p + by) % ranks * tensors + t % 2 * 2 + t // 2)
        for p in range(ranks)
        for t in range(tensors)
    ]
    return lax.ppermute(value, grid, pairs)


def from_twin(value):
    ranks = lax.axis_size("pipe")
    tensors = lax.axis_size("tensor")
    pairs = [
        (p * tensors + t, (p ^ 1) * tensors + (t ^ 2))
        for p in range(ranks)
        for t in range(tensors)
    ]
    return lax.ppermute(value, grid, pairs)


def from_replica(value, by):
    groups = lax.axis_size("dp")
    return lax.ppermute(value, "dp", [(i, (i + by) % groups) for i in range(groups)])


def gelu_pair(value):
    root = jnp.float32(0.7978845608028654)
    square = value * value
    inner = root * (value + 0.044715 * square * value)
    bend = jnp.tanh(inner)
    half = 0.5 * (1.0 + bend)
    slope = half + 0.5 * value * (1.0 - bend * bend) * root * (1.0 + 3 * 0.044715 * square)
    return value * half, slope


def whole_rows(piece, core):
    across = from_twin(piece)
    upper = lax.axis_index("tensor") // 2
    first = jnp.where(upper == 0, piece, across)
    second = jnp.where(upper == 0, across, piece)
    mine = jnp.concatenate([first, second], axis=1)
    theirs = from_core(mine)
    low = jnp.where(core == 0, mine, theirs)
    high = jnp.where(core == 0, theirs, mine)
    share = piece.shape[1]
    return jnp.concatenate(
        [low[:, :share], high[:, :share], low[:, share:], high[:, share:]], axis=1
    )


def send(part, by):
    theirs = from_core(part.astype(jnp.bfloat16))
    return to_rank((part + theirs.astype(jnp.float32)).astype(jnp.bfloat16), by)


def settle(come):
    return (come.astype(jnp.float32) + from_core(come).astype(jnp.float32)).astype(jnp.bfloat16)


def turn_block(from_ref, token_ref, to_ref):
    block = from_ref.shape[0]
    row = lax.broadcasted_iota(jnp.int32, (block, block), 0)
    column = lax.broadcasted_iota(jnp.int32, (block, block), 1)
    unit = jnp.where(row == column, 1.0, 0.0).astype(jnp.bfloat16)
    for first in range(0, from_ref.shape[1], block):
        to_ref[first : first + block, :] = lax.dot_general(
            unit,
            from_ref[:, first : first + block],
            contract_last,
            preferred_element_type=jnp.float32,
        ).astype(jnp.bfloat16)


def turned(weight, token, block):
    rows, columns = weight.shape
    return pl.pallas_call(
        turn_block,
        out_shape=jax.ShapeDtypeStruct((columns, rows), weight.dtype),
        grid=(rows // block,),
        in_specs=[
            pl.BlockSpec((block, columns), lambda i: (i, 0)),
            pl.BlockSpec(memory_space=pl.ANY),
        ],
        out_specs=pl.BlockSpec((columns, block), lambda i: (0, i)),
        compiler_params=pltpu.CompilerParams(vmem_limit_bytes=6 * 2**20),
        cost_estimate=pl.CostEstimate(
            flops=2 * rows * columns * block, bytes_accessed=4 * rows * columns, transcendentals=0
        ),
    )(weight, token)


def put(stack, item, index):
    return lax.dynamic_update_index_in_dim(stack, item, index, 0)


def take(stack, index):
    return lax.dynamic_index_in_dim(stack, index, 0, keepdims=False)


def terms(first, second, share):
    up_term = lax.dot_general(
        first[:, :share], second[:, share:], contract_first, preferred_element_type=jnp.float32
    )
    down_term = lax.dot_general(
        first[:, share:], second[:, :share], contract_first, preferred_element_type=jnp.float32
    )
    return up_term, down_term


def local(stream_a, stream_b, target_a, target_b, up_weight, down_weight):
    ranks = lax.axis_size("pipe")
    place = lax.axis_index("pipe")
    core = lax.axis_index("tensor") % 2
    groups = lax.axis_size("dp")
    member = lax.axis_index("dp")
    up = up_weight[0]
    down = down_weight[0]
    share = stream_a.shape[2]
    hid = up.shape[1]
    source = jnp.concatenate([stream_a, stream_b], axis=0).reshape(-1, share)
    source = whole_rows(source, core).reshape(CHUNKS, -1, MODEL_WIDTH)
    tokens = source.shape[1]
    stash = (
        jnp.zeros((CHUNKS + 1, tokens, 1), jnp.float32),
        jnp.zeros((CHUNKS + 1, tokens, MODEL_WIDTH), jnp.bfloat16),
        jnp.zeros((CHUNKS + 1, tokens, hid), jnp.bfloat16),
        jnp.zeros((CHUNKS + 1, tokens, hid), jnp.float32),
    )
    kept = (
        jnp.zeros((CHUNKS + 1, tokens, MODEL_WIDTH), jnp.bfloat16),
        jnp.zeros((CHUNKS + 1, tokens, hid), jnp.bfloat16),
    )
    steps = ranks + CHUNKS - 1
    rows = None
    grad = None
    waiting = None
    arrived = []
    half = CHUNKS // 2
    wave = half * tokens

    def cut(value, by):
        return lax.dynamic_slice_in_dim(value, ((member + by) % groups) * share, share, 1)

    def spread(wide, narrow):
        wide = wide.reshape(-1, MODEL_WIDTH)
        narrow = narrow.reshape(-1, hid)
        parts = []
        for by in range(groups):
            both = jnp.concatenate([cut(wide, by), narrow], axis=1)
            parts.append(from_replica(both, by) if by else both)
        return parts

    for step in range(steps + ranks - 1):
        turn = step - (ranks - 1)
        if step < steps:
            if step == 0:
                now = source[0]
            else:
                if step == 3:
                    rows, down_turned = lax.optimization_barrier((rows, down_turned))
                if step == 4:
                    rows, up_turned = lax.optimization_barrier((rows, up_turned))
                now = settle(rows)
                if step < CHUNKS:
                    now = jnp.where(place == 0, source[step], now)
            slot = jnp.clip(step - place, 0, CHUNKS)
            wide = now.astype(jnp.float32)
            scale = lax.rsqrt(jnp.mean(wide * wide, axis=1, keepdims=True) + epsilon)
            normed = (wide * scale).astype(jnp.bfloat16)
            if step == 1:
                target = jnp.concatenate([target_a, target_b], axis=0).reshape(-1, share)
                target, normed = lax.optimization_barrier((target, normed))
                target = whole_rows(target, core).reshape(CHUNKS, -1, MODEL_WIDTH)
            if step == 2:
                down_turned = turned(down, now, 256)
            if step == 3:
                up_turned = turned(up, now, 256)
            hidden = jnp.dot(normed, up, preferred_element_type=jnp.float32)
            active, slope = gelu_pair(hidden)
            active = active.astype(jnp.bfloat16)
            items = (scale, normed, active, slope)
            stash = tuple(put(stack, item, slot) for stack, item in zip(stash, items))
            if step < steps - 1:
                part = jnp.dot(active, down, preferred_element_type=jnp.float32) + 0.25 * wide
                rows = send(part, 1)
        if turn >= 0:
            if turn == 0:
                now = target[0]
            else:
                if waiting is not None:
                    grad, waiting = lax.optimization_barrier((grad, waiting))
                    arrived.append(waiting)
                    waiting = None
                now = settle(grad)
                if turn < CHUNKS:
                    now = jnp.where(place == ranks - 1, target[turn], now)
            slot = jnp.clip(turn - (ranks - 1 - place), 0, CHUNKS)
            back = jnp.dot(now, down_turned, preferred_element_type=jnp.float32)
            scale, normed, active, slope = (take(stack, slot) for stack in stash)
            delta = (back * slope).astype(jnp.bfloat16)
            kept = tuple(put(stack, item, slot) for stack, item in zip(kept, (now, delta)))
            if turn < steps - 1:
                push = jnp.dot(delta, up_turned, preferred_element_type=jnp.float32)
                unit = normed.astype(jnp.float32)
                inner = jnp.sum(push * unit, axis=1, keepdims=True) / MODEL_WIDTH
                part = 0.25 * now.astype(jnp.float32) + scale * (push - unit * inner)
                grad = send(part, -1)
            if step == steps:
                waiting = spread(stash[1][:half], stash[2][:half])
            if step == steps + 1:
                waiting = spread(stash[1][half:CHUNKS], stash[2][half:CHUNKS])
            if step == steps + ranks - 3:
                waiting = spread(kept[0][: CHUNKS - 1], kept[1][: CHUNKS - 1])
    arrived.append(spread(kept[0][CHUNKS - 1], kept[1][CHUNKS - 1]))
    first = jnp.concatenate(arrived[0] + arrived[1], axis=0)
    second = jnp.concatenate(
        [item[:wave] for item in arrived[2]]
        + [piece for pair in zip([item[wave:] for item in arrived[2]], arrived[3]) for piece in pair],
        axis=0,
    )
    up_sum, down_sum = terms(first, second, share)
    return (up_sum[None], down_sum[None])


def solution(mesh):
    return jax.shard_map(
        local,
        mesh=mesh,
        in_specs=(
            P("dp", None, "tensor"),
            P("dp", None, "tensor"),
            P("dp", None, "tensor"),
            P("dp", None, "tensor"),
            P("pipe", None, "tensor"),
            P("pipe", "tensor", None),
        ),
        out_specs=(P("pipe", "dp", "tensor"), P("pipe", "tensor", "dp")),
        check_vma=False,
    )
```

```python
import jax
import jax.numpy as jnp
from jax import lax
from jax.experimental import pallas as pl
from jax.experimental.pallas import tpu as pltpu
from jax.sharding import PartitionSpec as P

MODEL_WIDTH = 2048

CHUNKS = 4

epsilon = 1e-06
contract_last = (((1,), (1,)), ((), ()))
contract_first = (((0,), (0,)), ((), ()))
grid = ("pipe", "tensor")


def from_core(value):
    return lax.ppermute(value, "tensor", [(i, i ^ 1) for i in range(4)])


def to_rank(value, by):
    ranks = lax.axis_size("pipe")
    tensors = lax.axis_size("tensor")
    pairs = [
        (p * tensors + t, (p + by) % ranks * tensors + t % 2 * 2 + t // 2)
        for p in range(ranks)
        for t in range(tensors)
    ]
    return lax.ppermute(value, grid, pairs)


def from_twin(value):
    ranks = lax.axis_size("pipe")
    tensors = lax.axis_size("tensor")
    pairs = [
        (p * tensors + t, (p ^ 1) * tensors + (t ^ 2))
        for p in range(ranks)
        for t in range(tensors)
    ]
    return lax.ppermute(value, grid, pairs)


def from_replica(value, by):
    groups = lax.axis_size("dp")
    return lax.ppermute(value, "dp", [(i, (i + by) % groups) for i in range(groups)])


def gelu_pair(value):
    root = jnp.float32(0.7978845608028654)
    square = value * value
    inner = root * (value + 0.044715 * square * value)
    bend = jnp.tanh(inner)
    half = 0.5 * (1.0 + bend)
    slope = half + 0.5 * value * (1.0 - bend * bend) * root * (1.0 + 3 * 0.044715 * square)
    return value * half, slope


def whole_rows(piece, core):
    across = from_twin(piece)
    upper = lax.axis_index("tensor") // 2
    first = jnp.where(upper == 0, piece, across)
    second = jnp.where(upper == 0, across, piece)
    mine = jnp.concatenate([first, second], axis=1)
    theirs = from_core(mine)
    low = jnp.where(core == 0, mine, theirs)
    high = jnp.where(core == 0, theirs, mine)
    share = piece.shape[1]
    return jnp.concatenate(
        [low[:, :share], high[:, :share], low[:, share:], high[:, share:]], axis=1
    )


def send(parts, ways):
    tokens = parts[0].shape[0]
    theirs = from_core(jnp.concatenate([part.astype(jnp.bfloat16) for part in parts], axis=0))
    theirs = theirs.astype(jnp.float32)
    return [
        to_rank((part + theirs[i * tokens : (i + 1) * tokens]).astype(jnp.bfloat16), way)
        for i, (part, way) in enumerate(zip(parts, ways))
    ]


def settle(come):
    tokens = come[0].shape[0]
    theirs = from_core(jnp.concatenate(come, axis=0)).astype(jnp.float32)
    return [
        (item.astype(jnp.float32) + theirs[i * tokens : (i + 1) * tokens]).astype(jnp.bfloat16)
        for i, item in enumerate(come)
    ]


def turn_block(from_ref, token_ref, to_ref):
    block = from_ref.shape[0]
    row = lax.broadcasted_iota(jnp.int32, (block, block), 0)
    column = lax.broadcasted_iota(jnp.int32, (block, block), 1)
    unit = jnp.where(row == column, 1.0, 0.0).astype(jnp.bfloat16)
    for first in range(0, from_ref.shape[1], block):
        to_ref[first : first + block, :] = lax.dot_general(
            unit,
            from_ref[:, first : first + block],
            contract_last,
            preferred_element_type=jnp.float32,
        ).astype(jnp.bfloat16)


def turned(weight, token, block):
    rows, columns = weight.shape
    return pl.pallas_call(
        turn_block,
        out_shape=jax.ShapeDtypeStruct((columns, rows), weight.dtype),
        grid=(rows // block,),
        in_specs=[
            pl.BlockSpec((block, columns), lambda i: (i, 0)),
            pl.BlockSpec(memory_space=pl.ANY),
        ],
        out_specs=pl.BlockSpec((columns, block), lambda i: (0, i)),
        compiler_params=pltpu.CompilerParams(vmem_limit_bytes=6 * 2**20),
        cost_estimate=pl.CostEstimate(
            flops=2 * rows * columns * block, bytes_accessed=4 * rows * columns, transcendentals=0
        ),
    )(weight, token)


def put(stack, item, index):
    return lax.dynamic_update_index_in_dim(stack, item, index, 0)


def take(stack, index):
    return lax.dynamic_index_in_dim(stack, index, 0, keepdims=False)


def terms(first, second, share):
    up_term = lax.dot_general(
        first[:, :share], second[:, share:], contract_first, preferred_element_type=jnp.float32
    )
    down_term = lax.dot_general(
        first[:, share:], second[:, :share], contract_first, preferred_element_type=jnp.float32
    )
    return up_term, down_term


def local(stream_a, stream_b, target_a, target_b, up_weight, down_weight):
    ranks = lax.axis_size("pipe")
    place = lax.axis_index("pipe")
    core = lax.axis_index("tensor") % 2
    groups = lax.axis_size("dp")
    member = lax.axis_index("dp")
    up = up_weight[0]
    down = down_weight[0]
    share = stream_a.shape[2]
    hid = up.shape[1]
    source = jnp.concatenate([stream_a, stream_b], axis=0).reshape(-1, share)
    source = whole_rows(source, core).reshape(CHUNKS, -1, MODEL_WIDTH)
    tokens = source.shape[1]
    stash = (
        jnp.zeros((CHUNKS + 1, tokens, 1), jnp.float32),
        jnp.zeros((CHUNKS + 1, tokens, MODEL_WIDTH), jnp.bfloat16),
        jnp.zeros((CHUNKS + 1, tokens, hid), jnp.bfloat16),
        jnp.zeros((CHUNKS + 1, tokens, hid), jnp.float32),
    )
    kept = (
        jnp.zeros((CHUNKS + 1, tokens, MODEL_WIDTH), jnp.bfloat16),
        jnp.zeros((CHUNKS + 1, tokens, hid), jnp.bfloat16),
    )
    steps = ranks + CHUNKS - 1
    come = []
    coming = {}
    arrived = {}
    half = CHUNKS // 2
    early = slice(0, half)
    late = slice(half, CHUNKS)

    def cut(value, by):
        return lax.dynamic_slice_in_dim(value, ((member + by) % groups) * share, share, 1)

    def bundle(wide, narrow, which, by):
        wide = wide[which].reshape(-1, MODEL_WIDTH)
        narrow = narrow[which].reshape(-1, hid)
        return jnp.concatenate([cut(wide, by), narrow], axis=1)

    windows = {
        ranks: [("ahead", early, 1)],
        ranks + 1: [("ahead", early, 2)],
        ranks + 2: [("ahead", early, 3)],
        ranks + 3: [("ahead", late, 1)],
        ranks + 4: [("ahead", late, 2)],
        ranks + 5: [("ahead", late, 3)],
        steps + ranks - 4: [("behind", early, 1), ("behind", early, 3)],
        steps + ranks - 3: [("behind", early, 2)],
    }
    for step in range(steps + ranks - 1):
        turn = step - (ranks - 1)
        moving = step < steps
        held = []
        if step == 3:
            come[0], down_turned = lax.optimization_barrier((come[0], down_turned))
        if step == 4:
            come[0], up_turned = lax.optimization_barrier((come[0], up_turned))
        if coming:
            come, coming = lax.optimization_barrier((come, coming))
            arrived.update(coming)
            coming = {}
        if come:
            held = settle(come)
        parts = []
        ways = []
        if moving:
            if step == 0:
                now = source[0]
            else:
                now = held.pop(0)
                if step < CHUNKS:
                    now = jnp.where(place == 0, source[step], now)
            slot = jnp.clip(step - place, 0, CHUNKS)
            wide = now.astype(jnp.float32)
            scale = lax.rsqrt(jnp.mean(wide * wide, axis=1, keepdims=True) + epsilon)
            normed = (wide * scale).astype(jnp.bfloat16)
            if step == 1:
                target = jnp.concatenate([target_a, target_b], axis=0).reshape(-1, share)
                target, normed = lax.optimization_barrier((target, normed))
                target = whole_rows(target, core).reshape(CHUNKS, -1, MODEL_WIDTH)
            if step == 2:
                down_turned = turned(down, now, 256)
            if step == 3:
                up_turned = turned(up, now, 256)
            hidden = jnp.dot(normed, up, preferred_element_type=jnp.float32)
            active, slope = gelu_pair(hidden)
            active = active.astype(jnp.bfloat16)
            items = (scale, normed, active, slope)
            stash = tuple(put(stack, item, slot) for stack, item in zip(stash, items))
            if step < steps - 1:
                part = jnp.dot(active, down, preferred_element_type=jnp.float32) + 0.25 * wide
                parts.append(part)
                ways.append(1)
        if turn >= 0:
            if turn == 0:
                now = target[0]
            else:
                now = held.pop(0)
                if turn < CHUNKS:
                    now = jnp.where(place == ranks - 1, target[turn], now)
            slot = jnp.clip(turn - (ranks - 1 - place), 0, CHUNKS)
            back = jnp.dot(now, down_turned, preferred_element_type=jnp.float32)
            scale, normed, active, slope = (take(stack, slot) for stack in stash)
            delta = (back * slope).astype(jnp.bfloat16)
            kept = tuple(put(stack, item, slot) for stack, item in zip(kept, (now, delta)))
            if turn < steps - 1:
                push = jnp.dot(delta, up_turned, preferred_element_type=jnp.float32)
                unit = normed.astype(jnp.float32)
                inner = jnp.sum(push * unit, axis=1, keepdims=True) / MODEL_WIDTH
                part = 0.25 * now.astype(jnp.float32) + scale * (push - unit * inner)
                parts.append(part)
                ways.append(-1)
        if parts:
            come = send(parts, ways)
        for kind, which, by in windows.get(step, []):
            pair = (stash[1], stash[2]) if kind == "ahead" else kept
            name = kind + str(which.start) + str(by)
            coming[name] = from_replica(bundle(*pair, which, by), by)

    def gathered(kind, pair, which):
        pieces = [bundle(*pair, which, 0)]
        for by in range(1, groups):
            name = kind + str(which.start) + str(by)
            if name not in arrived:
                arrived[name] = from_replica(bundle(*pair, which, by), by)
            pieces.append(arrived[name])
        return pieces

    ahead = (stash[1], stash[2])
    first = gathered("ahead", ahead, early) + gathered("ahead", ahead, late)
    second = gathered("behind", kept, early) + gathered("behind", kept, late)
    first = jnp.concatenate(first, axis=0)
    second = jnp.concatenate(second, axis=0)
    up_sum, down_sum = terms(first, second, share)
    return (up_sum[None], down_sum[None])


def solution(mesh):
    return jax.shard_map(
        local,
        mesh=mesh,
        in_specs=(
            P("dp", None, "tensor"),
            P("dp", None, "tensor"),
            P("dp", None, "tensor"),
            P("dp", None, "tensor"),
            P("pipe", None, "tensor"),
            P("pipe", "tensor", None),
        ),
        out_specs=(P("pipe", "dp", "tensor"), P("pipe", "tensor", "dp")),
        check_vma=False,
    )
```

```python
import jax
import jax.numpy as jnp
from jax import lax
from jax.experimental import pallas as pl
from jax.experimental.pallas import tpu as pltpu
from jax.sharding import PartitionSpec as P

MODEL_WIDTH = 2048

CHUNKS = 4

epsilon = 1e-06
contract_last = (((1,), (1,)), ((), ()))
contract_first = (((0,), (0,)), ((), ()))
grid = ("pipe", "tensor")


def from_core(value):
    return lax.ppermute(value, "tensor", [(i, i ^ 1) for i in range(4)])


def to_rank(value, path):
    ranks = lax.axis_size("pipe")
    tensors = lax.axis_size("tensor")
    step = 1 if path[1] > path[0] else -1
    if len(path) > 4:
        path = [p % ranks for p in range(0, step * ranks, step)]
    after = {p: path[(i + 1) % len(path)] for i, p in enumerate(path)}
    pairs = []
    for p in range(ranks):
        there = after.get(p, p if p ^ 1 in after else p ^ 1)
        for t in range(tensors):
            other = t ^ 1 if there == p else t % 2 * 2 + t // 2
            pairs.append((p * tensors + t, there * tensors + other))
    return lax.ppermute(value, grid, pairs)


def from_twin(value):
    ranks = lax.axis_size("pipe")
    tensors = lax.axis_size("tensor")
    pairs = [
        (p * tensors + t, (p ^ 1) * tensors + (t ^ 2))
        for p in range(ranks)
        for t in range(tensors)
    ]
    return lax.ppermute(value, grid, pairs)


def from_replica(value, by):
    groups = lax.axis_size("dp")
    return lax.ppermute(value, "dp", [(i, (i + by) % groups) for i in range(groups)])


def gelu_pair(value):
    root = jnp.float32(0.7978845608028654)
    square = value * value
    inner = root * (value + 0.044715 * square * value)
    bend = jnp.tanh(inner)
    half = 0.5 * (1.0 + bend)
    slope = half + 0.5 * value * (1.0 - bend * bend) * root * (1.0 + 3 * 0.044715 * square)
    return value * half, slope


def whole_rows(piece, core):
    across = from_twin(piece)
    upper = lax.axis_index("tensor") // 2
    first = jnp.where(upper == 0, piece, across)
    second = jnp.where(upper == 0, across, piece)
    mine = jnp.concatenate([first, second], axis=1)
    theirs = from_core(mine)
    low = jnp.where(core == 0, mine, theirs)
    high = jnp.where(core == 0, theirs, mine)
    share = piece.shape[1]
    return jnp.concatenate(
        [low[:, :share], high[:, :share], low[:, share:], high[:, share:]], axis=1
    )


def send(parts, paths):
    tokens = parts[0].shape[0]
    theirs = from_core(jnp.concatenate([part.astype(jnp.bfloat16) for part in parts], axis=0))
    come = []
    for i, (part, path) in enumerate(zip(parts, paths)):
        other = theirs[i * tokens : (i + 1) * tokens].astype(jnp.float32)
        come.append(to_rank((part + other).astype(jnp.bfloat16), path))
    return come


def settle(come):
    tokens = come[0].shape[0]
    theirs = from_core(jnp.concatenate(come, axis=0))
    held = []
    for i, item in enumerate(come):
        other = theirs[i * tokens : (i + 1) * tokens].astype(jnp.float32)
        held.append((item.astype(jnp.float32) + other).astype(jnp.bfloat16))
    return held


def turn_block(from_ref, token_ref, to_ref):
    block = from_ref.shape[0]
    row = lax.broadcasted_iota(jnp.int32, (block, block), 0)
    column = lax.broadcasted_iota(jnp.int32, (block, block), 1)
    unit = jnp.where(row == column, 1.0, 0.0).astype(jnp.bfloat16)
    for first in range(0, from_ref.shape[1], block):
        to_ref[first : first + block, :] = lax.dot_general(
            unit,
            from_ref[:, first : first + block],
            contract_last,
            preferred_element_type=jnp.float32,
        ).astype(jnp.bfloat16)


def turned(weight, token, block):
    rows, columns = weight.shape
    return pl.pallas_call(
        turn_block,
        out_shape=jax.ShapeDtypeStruct((columns, rows), weight.dtype),
        grid=(rows // block,),
        in_specs=[
            pl.BlockSpec((block, columns), lambda i: (i, 0)),
            pl.BlockSpec(memory_space=pl.ANY),
        ],
        out_specs=pl.BlockSpec((columns, block), lambda i: (0, i)),
        compiler_params=pltpu.CompilerParams(vmem_limit_bytes=6 * 2**20),
        cost_estimate=pl.CostEstimate(
            flops=2 * rows * columns * block, bytes_accessed=4 * rows * columns, transcendentals=0
        ),
    )(weight, token)


def put(stack, item, index):
    return lax.dynamic_update_index_in_dim(stack, item, index, 0)


def take(stack, index):
    return lax.dynamic_index_in_dim(stack, index, 0, keepdims=False)


def terms(first, second, share):
    up_term = lax.dot_general(
        first[:, :share], second[:, share:], contract_first, preferred_element_type=jnp.float32
    )
    down_term = lax.dot_general(
        first[:, share:], second[:, :share], contract_first, preferred_element_type=jnp.float32
    )
    return up_term, down_term


def local(stream_a, stream_b, target_a, target_b, up_weight, down_weight):
    ranks = lax.axis_size("pipe")
    place = lax.axis_index("pipe")
    core = lax.axis_index("tensor") % 2
    groups = lax.axis_size("dp")
    member = lax.axis_index("dp")
    up = up_weight[0]
    down = down_weight[0]
    share = stream_a.shape[2]
    half = CHUNKS // 2
    hid = up.shape[1]
    source = [
        whole_rows(stream.reshape(-1, share), core).reshape(half, -1, MODEL_WIDTH)
        for stream in (stream_a, stream_b)
    ]
    source = [piece[i] for piece in source for i in range(half)]
    tokens = source[0].shape[0]
    stash = (
        jnp.zeros((CHUNKS + 1, tokens, 1), jnp.float32),
        jnp.zeros((CHUNKS + 1, tokens, MODEL_WIDTH), jnp.bfloat16),
        jnp.zeros((CHUNKS + 1, tokens, hid), jnp.bfloat16),
        jnp.zeros((CHUNKS + 1, tokens, hid), jnp.float32),
    )
    kept = (
        jnp.zeros((CHUNKS + 1, tokens, MODEL_WIDTH), jnp.bfloat16),
        jnp.zeros((CHUNKS + 1, tokens, hid), jnp.bfloat16),
    )
    steps = ranks + CHUNKS - 1
    come = []
    coming = {}
    arrived = {}
    early = slice(0, half)
    late = slice(half, CHUNKS)

    def cut(value, by):
        return lax.dynamic_slice_in_dim(value, ((member + by) % groups) * share, share, 1)

    def bundle(wide, narrow, which, by):
        wide = wide[which].reshape(-1, MODEL_WIDTH)
        narrow = narrow[which].reshape(-1, hid)
        return jnp.concatenate([cut(wide, by), narrow], axis=1)

    windows = {
        ranks: [("ahead", early, 1)],
        ranks + 1: [("ahead", early, 2)],
        ranks + 2: [("ahead", early, 3)],
        ranks + 3: [("ahead", late, 1)],
        ranks + 4: [("ahead", late, 2)],
        ranks + 5: [("ahead", late, 3)],
        steps + ranks - 4: [("behind", early, 1), ("behind", early, 3)],
        steps + ranks - 3: [("behind", early, 2)],
    }
    for step in range(steps + ranks - 1):
        turn = step - (ranks - 1)
        moving = step < steps
        held = []
        if step == 3:
            come[0], down_turned = lax.optimization_barrier((come[0], down_turned))
        if step == 4:
            come[0], up_turned = lax.optimization_barrier((come[0], up_turned))
        if coming:
            come, coming = lax.optimization_barrier((come, coming))
            arrived.update(coming)
            coming = {}
        if come:
            held = settle(come)
        parts = []
        ways = []
        if moving:
            if step == 0:
                now = source[0]
            else:
                now = held.pop(0)
                if step < CHUNKS:
                    now = jnp.where(place == 0, source[step], now)
            slot = jnp.clip(step - place, 0, CHUNKS)
            wide = now.astype(jnp.float32)
            scale = lax.rsqrt(jnp.mean(wide * wide, axis=1, keepdims=True) + epsilon)
            normed = (wide * scale).astype(jnp.bfloat16)
            if step == 1:
                late_a, late_b, normed = lax.optimization_barrier((target_a, target_b, normed))
                target = [
                    whole_rows(item.reshape(-1, share), core).reshape(half, -1, MODEL_WIDTH)
                    for item in (late_a, late_b)
                ]
                target = [piece[i] for piece in target for i in range(half)]
            if step == 2:
                down_turned = turned(down, now, 256)
            if step == 3:
                up_turned = turned(up, now, 256)
            hidden = jnp.dot(normed, up, preferred_element_type=jnp.float32)
            active, slope = gelu_pair(hidden)
            active = active.astype(jnp.bfloat16)
            items = (scale, normed, active, slope)
            stash = tuple(put(stack, item, slot) for stack, item in zip(stash, items))
            if step < steps - 1:
                part = jnp.dot(active, down, preferred_element_type=jnp.float32) + 0.25 * wide
                parts.append(part)
                ways.append(range(max(0, step - CHUNKS + 1), min(ranks, step + 2)))
        if turn >= 0:
            if turn == 0:
                now = target[0]
            else:
                now = held.pop(0)
                if turn < CHUNKS:
                    now = jnp.where(place == ranks - 1, target[turn], now)
            slot = jnp.clip(turn - (ranks - 1 - place), 0, CHUNKS)
            back = jnp.dot(now, down_turned, preferred_element_type=jnp.float32)
            scale, normed, active, slope = (take(stack, slot) for stack in stash)
            delta = (back * slope).astype(jnp.bfloat16)
            kept = tuple(put(stack, item, slot) for stack, item in zip(kept, (now, delta)))
            if turn < steps - 1:
                push = jnp.dot(delta, up_turned, preferred_element_type=jnp.float32)
                unit = normed.astype(jnp.float32)
                inner = jnp.sum(push * unit, axis=1, keepdims=True) / MODEL_WIDTH
                part = 0.25 * now.astype(jnp.float32) + scale * (push - unit * inner)
                parts.append(part)
                most = min(ranks - 1, ranks - 2 - turn + CHUNKS)
                ways.append(range(most, max(-1, ranks - 3 - turn), -1))
        if parts:
            come = send(parts, ways)
        for kind, which, by in windows.get(step, []):
            pair = (stash[1], stash[2]) if kind == "ahead" else kept
            name = kind + str(which.start) + str(by)
            coming[name] = from_replica(bundle(*pair, which, by), by)

    def gathered(kind, pair, which):
        pieces = [bundle(*pair, which, 0)]
        for by in range(1, groups):
            name = kind + str(which.start) + str(by)
            if name not in arrived:
                arrived[name] = from_replica(bundle(*pair, which, by), by)
            pieces.append(arrived[name])
        return pieces

    ahead = (stash[1], stash[2])
    first = gathered("ahead", ahead, early) + gathered("ahead", ahead, late)
    second = gathered("behind", kept, early) + gathered("behind", kept, late)
    first = jnp.concatenate(first, axis=0)
    second = jnp.concatenate(second, axis=0)
    up_sum, down_sum = terms(first, second, share)
    return (up_sum[None], down_sum[None])


def solution(mesh):
    return jax.shard_map(
        local,
        mesh=mesh,
        in_specs=(
            P("dp", None, "tensor"),
            P("dp", None, "tensor"),
            P("dp", None, "tensor"),
            P("dp", None, "tensor"),
            P("pipe", None, "tensor"),
            P("pipe", "tensor", None),
        ),
        out_specs=(P("pipe", "dp", "tensor"), P("pipe", "tensor", "dp")),
        check_vma=False,
    )
```

```python
import jax
import jax.numpy as jnp
from jax import lax
from jax.experimental import pallas as pl
from jax.experimental.pallas import tpu as pltpu
from jax.sharding import PartitionSpec as P

MODEL_WIDTH = 2048

CHUNKS = 4

epsilon = 1e-06
contract_last = (((1,), (1,)), ((), ()))
contract_first = (((0,), (0,)), ((), ()))
grid = ("pipe", "tensor")


def from_core(value):
    return lax.ppermute(value, "tensor", [(i, i ^ 1) for i in range(4)])


def to_rank(value, path):
    ranks = lax.axis_size("pipe")
    tensors = lax.axis_size("tensor")
    after = {p: path[(i + 1) % len(path)] for i, p in enumerate(path)}
    pairs = []
    for p in range(ranks):
        there = after.get(p, p if p ^ 1 in after else p ^ 1)
        for t in range(tensors):
            if there == p:
                other = t ^ 1
            elif p == path[-1] and len(path) > 2:
                other = t
            else:
                other = t % 2 * 2 + t // 2
            pairs.append((p * tensors + t, there * tensors + other))
    return lax.ppermute(value, grid, pairs)


def from_twin(value):
    ranks = lax.axis_size("pipe")
    tensors = lax.axis_size("tensor")
    pairs = [
        (p * tensors + t, (p ^ 1) * tensors + (t ^ 2))
        for p in range(ranks)
        for t in range(tensors)
    ]
    return lax.ppermute(value, grid, pairs)


def from_replica(value, by):
    groups = lax.axis_size("dp")
    return lax.ppermute(value, "dp", [(i, (i + by) % groups) for i in range(groups)])


def gelu_pair(value):
    root = jnp.float32(0.7978845608028654)
    square = value * value
    inner = root * (value + 0.044715 * square * value)
    bend = jnp.tanh(inner)
    half = 0.5 * (1.0 + bend)
    slope = half + 0.5 * value * (1.0 - bend * bend) * root * (1.0 + 3 * 0.044715 * square)
    return value * half, slope


def whole_rows(piece, core):
    across = from_twin(piece)
    upper = lax.axis_index("tensor") // 2
    first = jnp.where(upper == 0, piece, across)
    second = jnp.where(upper == 0, across, piece)
    mine = jnp.concatenate([first, second], axis=1)
    theirs = from_core(mine)
    low = jnp.where(core == 0, mine, theirs)
    high = jnp.where(core == 0, theirs, mine)
    share = piece.shape[1]
    return jnp.concatenate(
        [low[:, :share], high[:, :share], low[:, share:], high[:, share:]], axis=1
    )


def send(parts, paths):
    tokens = parts[0].shape[0]
    theirs = from_core(jnp.concatenate([part.astype(jnp.bfloat16) for part in parts], axis=0))
    come = []
    for i, (part, path) in enumerate(zip(parts, paths)):
        other = theirs[i * tokens : (i + 1) * tokens].astype(jnp.float32)
        come.append(to_rank((part + other).astype(jnp.bfloat16), path))
    return come


def settle(come):
    tokens = come[0].shape[0]
    theirs = from_core(jnp.concatenate(come, axis=0))
    held = []
    for i, item in enumerate(come):
        other = theirs[i * tokens : (i + 1) * tokens].astype(jnp.float32)
        held.append((item.astype(jnp.float32) + other).astype(jnp.bfloat16))
    return held


def turn_block(from_ref, token_ref, to_ref):
    block = from_ref.shape[0]
    row = lax.broadcasted_iota(jnp.int32, (block, block), 0)
    column = lax.broadcasted_iota(jnp.int32, (block, block), 1)
    unit = jnp.where(row == column, 1.0, 0.0).astype(jnp.bfloat16)
    for first in range(0, from_ref.shape[1], block):
        to_ref[first : first + block, :] = lax.dot_general(
            unit,
            from_ref[:, first : first + block],
            contract_last,
            preferred_element_type=jnp.float32,
        ).astype(jnp.bfloat16)


def turned(weight, token, block):
    rows, columns = weight.shape
    return pl.pallas_call(
        turn_block,
        out_shape=jax.ShapeDtypeStruct((columns, rows), weight.dtype),
        grid=(rows // block,),
        in_specs=[
            pl.BlockSpec((block, columns), lambda i: (i, 0)),
            pl.BlockSpec(memory_space=pl.ANY),
        ],
        out_specs=pl.BlockSpec((columns, block), lambda i: (0, i)),
        compiler_params=pltpu.CompilerParams(vmem_limit_bytes=6 * 2**20),
        cost_estimate=pl.CostEstimate(
            flops=2 * rows * columns * block, bytes_accessed=4 * rows * columns, transcendentals=0
        ),
    )(weight, token)


def put(stack, item, index):
    return lax.dynamic_update_index_in_dim(stack, item, index, 0)


def take(stack, index):
    return lax.dynamic_index_in_dim(stack, index, 0, keepdims=False)


def terms(first, second, share):
    up_term = lax.dot_general(
        first[:, :share], second[:, share:], contract_first, preferred_element_type=jnp.float32
    )
    down_term = lax.dot_general(
        first[:, share:], second[:, :share], contract_first, preferred_element_type=jnp.float32
    )
    return up_term, down_term


def local(stream_a, stream_b, target_a, target_b, up_weight, down_weight):
    ranks = lax.axis_size("pipe")
    place = lax.axis_index("pipe")
    core = lax.axis_index("tensor") % 2
    groups = lax.axis_size("dp")
    member = lax.axis_index("dp")
    up = up_weight[0]
    down = down_weight[0]
    share = stream_a.shape[2]
    half = CHUNKS // 2
    hid = up.shape[1]
    flat = lambda value: value.reshape(-1, share)
    source = whole_rows(flat(stream_a), core).reshape(half, -1, MODEL_WIDTH)
    others = jnp.concatenate([flat(item) for item in (stream_b, target_a, target_b)], axis=0)
    others = whole_rows(others, core).reshape(3 * half, -1, MODEL_WIDTH)
    source = [source[i] for i in range(half)] + [others[i] for i in range(half)]
    target = [others[i] for i in range(half, 3 * half)]
    tokens = source[0].shape[0]
    stash = (
        jnp.zeros((CHUNKS + 1, tokens, 1), jnp.float32),
        jnp.zeros((CHUNKS + 1, tokens, MODEL_WIDTH), jnp.bfloat16),
        jnp.zeros((CHUNKS + 1, tokens, hid), jnp.bfloat16),
        jnp.zeros((CHUNKS + 1, tokens, hid), jnp.float32),
    )
    kept = (
        jnp.zeros((CHUNKS + 1, tokens, MODEL_WIDTH), jnp.bfloat16),
        jnp.zeros((CHUNKS + 1, tokens, hid), jnp.bfloat16),
    )
    steps = ranks + CHUNKS - 1
    come = []
    coming = {}
    arrived = {}
    early = slice(0, half)
    late = slice(half, CHUNKS)

    def cut(value, by):
        return lax.dynamic_slice_in_dim(value, ((member + by) % groups) * share, share, 1)

    def bundle(wide, narrow, which, by):
        wide = wide[which].reshape(-1, MODEL_WIDTH)
        narrow = narrow[which].reshape(-1, hid)
        return jnp.concatenate([cut(wide, by), narrow], axis=1)

    windows = {
        steps - 1: [("ahead", early, 1)],
        steps: [("ahead", early, 2)],
        steps + 1: [("ahead", early, 3)],
        steps + 2: [("ahead", late, 1)],
        steps + 3: [("ahead", late, 2), ("ahead", late, 3)],
        steps + ranks - 4: [("behind", early, 1), ("behind", early, 3)],
        steps + ranks - 3: [("behind", early, 2)],
    }
    for step in range(steps + ranks - 1):
        turn = step - (ranks - 1)
        moving = step < steps
        held = []
        if step == 3:
            come[0], down_turned = lax.optimization_barrier((come[0], down_turned))
        if step == 4:
            come[0], up_turned = lax.optimization_barrier((come[0], up_turned))
        if coming:
            come, coming = lax.optimization_barrier((come, coming))
            arrived.update(coming)
            coming = {}
        if come:
            held = settle(come)
        parts = []
        ways = []
        if moving:
            if step == 0:
                now = source[0]
            else:
                now = held.pop(0)
                if step < CHUNKS:
                    now = jnp.where(place == 0, source[step], now)
            slot = jnp.clip(step - place, 0, CHUNKS)
            wide = now.astype(jnp.float32)
            scale = lax.rsqrt(jnp.mean(wide * wide, axis=1, keepdims=True) + epsilon)
            normed = (wide * scale).astype(jnp.bfloat16)
            if step == 2:
                down_turned = turned(down, now, 256)
            if step == 3:
                up_turned = turned(up, now, 256)
            hidden = jnp.dot(normed, up, preferred_element_type=jnp.float32)
            active, slope = gelu_pair(hidden)
            active = active.astype(jnp.bfloat16)
            items = (scale, normed, active, slope)
            stash = tuple(put(stack, item, slot) for stack, item in zip(stash, items))
            if step < steps - 1:
                part = jnp.dot(active, down, preferred_element_type=jnp.float32) + 0.25 * wide
                parts.append(part)
                ways.append(range(max(0, step - CHUNKS + 1), min(ranks, step + 2)))
        if turn >= 0:
            if turn == 0:
                now = target[0]
            else:
                now = held.pop(0)
                if turn < CHUNKS:
                    now = jnp.where(place == ranks - 1, target[turn], now)
            slot = jnp.clip(turn - (ranks - 1 - place), 0, CHUNKS)
            back = jnp.dot(now, down_turned, preferred_element_type=jnp.float32)
            scale, normed, active, slope = (take(stack, slot) for stack in stash)
            delta = (back * slope).astype(jnp.bfloat16)
            kept = tuple(put(stack, item, slot) for stack, item in zip(kept, (now, delta)))
            if turn < steps - 1:
                push = jnp.dot(delta, up_turned, preferred_element_type=jnp.float32)
                unit = normed.astype(jnp.float32)
                inner = jnp.sum(push * unit, axis=1, keepdims=True) / MODEL_WIDTH
                part = 0.25 * now.astype(jnp.float32) + scale * (push - unit * inner)
                parts.append(part)
                most = min(ranks - 1, ranks - 2 - turn + CHUNKS)
                ways.append(range(most, max(-1, ranks - 3 - turn), -1))
        if parts:
            come = send(parts, ways)
        for kind, which, by in windows.get(step, []):
            pair = (stash[1], stash[2]) if kind == "ahead" else kept
            name = kind + str(which.start) + str(by)
            coming[name] = from_replica(bundle(*pair, which, by), by)

    def gathered(kind, pair, which):
        pieces = [bundle(*pair, which, 0)]
        for by in range(1, groups):
            name = kind + str(which.start) + str(by)
            if name not in arrived:
                arrived[name] = from_replica(bundle(*pair, which, by), by)
            pieces.append(arrived[name])
        return pieces

    ahead = (stash[1], stash[2])
    first = gathered("ahead", ahead, early) + gathered("ahead", ahead, late)
    second = gathered("behind", kept, early) + gathered("behind", kept, late)
    first = jnp.concatenate(first, axis=0)
    second = jnp.concatenate(second, axis=0)
    up_sum, down_sum = terms(first, second, share)
    return (up_sum[None], down_sum[None])


def solution(mesh):
    return jax.shard_map(
        local,
        mesh=mesh,
        in_specs=(
            P("dp", None, "tensor"),
            P("dp", None, "tensor"),
            P("dp", None, "tensor"),
            P("dp", None, "tensor"),
            P("pipe", None, "tensor"),
            P("pipe", "tensor", None),
        ),
        out_specs=(P("pipe", "dp", "tensor"), P("pipe", "tensor", "dp")),
        check_vma=False,
    )
```

```python
import jax
import jax.numpy as jnp
from jax import lax
from jax.experimental import pallas as pl
from jax.experimental.pallas import tpu as pltpu
from jax.sharding import PartitionSpec as P

MODEL_WIDTH = 2048

CHUNKS = 4

epsilon = 1e-06
contract_last = (((1,), (1,)), ((), ()))
contract_first = (((0,), (0,)), ((), ()))
grid = ("pipe", "tensor")


def from_core(value):
    return lax.ppermute(value, "tensor", [(i, i ^ 1) for i in range(4)])


def to_rank(value, path):
    ranks = lax.axis_size("pipe")
    tensors = lax.axis_size("tensor")
    after = {p: path[(i + 1) % len(path)] for i, p in enumerate(path)}
    pairs = []
    for p in range(ranks):
        there = after.get(p, p if p ^ 1 in after else p ^ 1)
        for t in range(tensors):
            if there == p:
                other = t ^ 1
            elif p == path[-1] and len(path) > 2:
                other = t
            else:
                other = t % 2 * 2 + t // 2
            pairs.append((p * tensors + t, there * tensors + other))
    return lax.ppermute(value, grid, pairs)


def from_twin(value):
    ranks = lax.axis_size("pipe")
    tensors = lax.axis_size("tensor")
    pairs = [
        (p * tensors + t, (p ^ 1) * tensors + (t ^ 2))
        for p in range(ranks)
        for t in range(tensors)
    ]
    return lax.ppermute(value, grid, pairs)


def from_replica(value, by):
    groups = lax.axis_size("dp")
    return lax.ppermute(value, "dp", [(i, (i + by) % groups) for i in range(groups)])


def gelu_pair(value):
    root = jnp.float32(0.7978845608028654)
    square = value * value
    inner = root * (value + 0.044715 * square * value)
    bend = jnp.tanh(inner)
    half = 0.5 * (1.0 + bend)
    slope = half + 0.5 * value * (1.0 - bend * bend) * root * (1.0 + 3 * 0.044715 * square)
    return value * half, slope


def whole_rows(piece, core):
    across = from_twin(piece)
    upper = lax.axis_index("tensor") // 2
    first = jnp.where(upper == 0, piece, across)
    second = jnp.where(upper == 0, across, piece)
    mine = jnp.concatenate([first, second], axis=1)
    theirs = from_core(mine)
    low = jnp.where(core == 0, mine, theirs)
    high = jnp.where(core == 0, theirs, mine)
    share = piece.shape[1]
    return jnp.concatenate(
        [low[:, :share], high[:, :share], low[:, share:], high[:, share:]], axis=1
    )


def send(parts, paths):
    tokens = parts[0].shape[0]
    theirs = from_core(jnp.concatenate([part.astype(jnp.bfloat16) for part in parts], axis=0))
    come = []
    for i, (part, path) in enumerate(zip(parts, paths)):
        other = theirs[i * tokens : (i + 1) * tokens].astype(jnp.float32)
        come.append(to_rank((part + other).astype(jnp.bfloat16), path))
    return come


def settle(come):
    held = []
    for item in come:
        other = from_core(item).astype(jnp.float32)
        held.append((item.astype(jnp.float32) + other).astype(jnp.bfloat16))
    return held


def turn_block(from_ref, token_ref, to_ref):
    block = from_ref.shape[0]
    row = lax.broadcasted_iota(jnp.int32, (block, block), 0)
    column = lax.broadcasted_iota(jnp.int32, (block, block), 1)
    unit = jnp.where(row == column, 1.0, 0.0).astype(jnp.bfloat16)
    for first in range(0, from_ref.shape[1], block):
        to_ref[first : first + block, :] = lax.dot_general(
            unit,
            from_ref[:, first : first + block],
            contract_last,
            preferred_element_type=jnp.float32,
        ).astype(jnp.bfloat16)


def turned(weight, token, block):
    rows, columns = weight.shape
    return pl.pallas_call(
        turn_block,
        out_shape=jax.ShapeDtypeStruct((columns, rows), weight.dtype),
        grid=(rows // block,),
        in_specs=[
            pl.BlockSpec((block, columns), lambda i: (i, 0)),
            pl.BlockSpec(memory_space=pl.ANY),
        ],
        out_specs=pl.BlockSpec((columns, block), lambda i: (0, i)),
        compiler_params=pltpu.CompilerParams(vmem_limit_bytes=6 * 2**20),
        cost_estimate=pl.CostEstimate(
            flops=2 * rows * columns * block, bytes_accessed=4 * rows * columns, transcendentals=0
        ),
    )(weight, token)


def put(stack, item, index):
    return lax.dynamic_update_index_in_dim(stack, item, index, 0)


def take(stack, index):
    return lax.dynamic_index_in_dim(stack, index, 0, keepdims=False)


def terms(first, second, share):
    up_term = lax.dot_general(
        first[:, :share], second[:, share:], contract_first, preferred_element_type=jnp.float32
    )
    down_term = lax.dot_general(
        first[:, share:], second[:, :share], contract_first, preferred_element_type=jnp.float32
    )
    return up_term, down_term


def local(stream_a, stream_b, target_a, target_b, up_weight, down_weight):
    ranks = lax.axis_size("pipe")
    place = lax.axis_index("pipe")
    core = lax.axis_index("tensor") % 2
    groups = lax.axis_size("dp")
    member = lax.axis_index("dp")
    up = up_weight[0]
    down = down_weight[0]
    share = stream_a.shape[2]
    half = CHUNKS // 2
    hid = up.shape[1]
    flat = lambda value: value.reshape(-1, share)
    source = whole_rows(flat(stream_a), core).reshape(half, -1, MODEL_WIDTH)
    others = jnp.concatenate([flat(item) for item in (stream_b, target_a, target_b)], axis=0)
    others = whole_rows(others, core).reshape(3 * half, -1, MODEL_WIDTH)
    source = [source[i] for i in range(half)] + [others[i] for i in range(half)]
    target = [others[i] for i in range(half, 3 * half)]
    tokens = source[0].shape[0]
    stash = (
        jnp.zeros((CHUNKS + 1, tokens, 1), jnp.float32),
        jnp.zeros((CHUNKS + 1, tokens, MODEL_WIDTH), jnp.bfloat16),
        jnp.zeros((CHUNKS + 1, tokens, hid), jnp.bfloat16),
        jnp.zeros((CHUNKS + 1, tokens, hid), jnp.float32),
    )
    kept = (
        jnp.zeros((CHUNKS + 1, tokens, MODEL_WIDTH), jnp.bfloat16),
        jnp.zeros((CHUNKS + 1, tokens, hid), jnp.bfloat16),
    )
    steps = ranks + CHUNKS - 1
    come = []
    coming = {}
    arrived = {}

    def cut(value, by):
        return lax.dynamic_slice_in_dim(value, ((member + by) % groups) * share, share, 1)

    def bundle(wide, narrow, by):
        wide = wide[:CHUNKS].reshape(-1, MODEL_WIDTH)
        narrow = narrow[:CHUNKS].reshape(-1, hid)
        return jnp.concatenate([cut(wide, by), narrow], axis=1)

    windows = {
        steps - 1: [1],
        steps: [2],
        steps + 1: [3],
    }
    for step in range(steps + ranks - 1):
        turn = step - (ranks - 1)
        moving = step < steps
        held = []
        if step == 3:
            come[0], down_turned = lax.optimization_barrier((come[0], down_turned))
        if step == 4:
            come[0], up_turned = lax.optimization_barrier((come[0], up_turned))
        if coming:
            come, coming = lax.optimization_barrier((come, coming))
            arrived.update(coming)
            coming = {}
        if come:
            held = settle(come)
        parts = []
        ways = []
        if moving:
            if step == 0:
                now = source[0]
            else:
                now = held.pop(0)
                if step < CHUNKS:
                    now = jnp.where(place == 0, source[step], now)
            slot = jnp.clip(step - place, 0, CHUNKS)
            wide = now.astype(jnp.float32)
            scale = lax.rsqrt(jnp.mean(wide * wide, axis=1, keepdims=True) + epsilon)
            normed = (wide * scale).astype(jnp.bfloat16)
            if step == 2:
                down_turned = turned(down, now, 256)
            if step == 3:
                up_turned = turned(up, now, 256)
            hidden = jnp.dot(normed, up, preferred_element_type=jnp.float32)
            active, slope = gelu_pair(hidden)
            active = active.astype(jnp.bfloat16)
            items = (scale, normed, active, slope)
            stash = tuple(put(stack, item, slot) for stack, item in zip(stash, items))
            if step < steps - 1:
                part = jnp.dot(active, down, preferred_element_type=jnp.float32) + 0.25 * wide
                parts.append(part)
                ways.append(range(max(0, step - CHUNKS + 1), min(ranks, step + 2)))
        if turn >= 0:
            if turn == 0:
                now = target[0]
            else:
                now = held.pop(0)
                if turn < CHUNKS:
                    now = jnp.where(place == ranks - 1, target[turn], now)
            slot = jnp.clip(turn - (ranks - 1 - place), 0, CHUNKS)
            back = jnp.dot(now, down_turned, preferred_element_type=jnp.float32)
            scale, normed, active, slope = (take(stack, slot) for stack in stash)
            delta = (back * slope).astype(jnp.bfloat16)
            kept = tuple(put(stack, item, slot) for stack, item in zip(kept, (now, delta)))
            if turn < steps - 1:
                push = jnp.dot(delta, up_turned, preferred_element_type=jnp.float32)
                unit = normed.astype(jnp.float32)
                inner = jnp.sum(push * unit, axis=1, keepdims=True) / MODEL_WIDTH
                part = 0.25 * now.astype(jnp.float32) + scale * (push - unit * inner)
                parts.append(part)
                most = min(ranks - 1, ranks - 2 - turn + CHUNKS)
                ways.append(range(most, max(-1, ranks - 3 - turn), -1))
        if parts:
            come = send(parts, ways)
        for by in windows.get(step, []):
            coming[by] = from_replica(bundle(stash[1], stash[2], by), by)
    first = [bundle(stash[1], stash[2], 0)] + [arrived[by] for by in range(1, groups)]
    second = [bundle(*kept, 0)]
    for by in range(1, groups):
        second.append(from_replica(bundle(*kept, by), by))
    first = jnp.concatenate(first, axis=0)
    second = jnp.concatenate(second, axis=0)
    up_sum, down_sum = terms(first, second, share)
    return (up_sum[None], down_sum[None])


def solution(mesh):
    return jax.shard_map(
        local,
        mesh=mesh,
        in_specs=(
            P("dp", None, "tensor"),
            P("dp", None, "tensor"),
            P("dp", None, "tensor"),
            P("dp", None, "tensor"),
            P("pipe", None, "tensor"),
            P("pipe", "tensor", None),
        ),
        out_specs=(P("pipe", "dp", "tensor"), P("pipe", "tensor", "dp")),
        check_vma=False,
    )
```

```python
import jax
import jax.numpy as jnp
from jax import lax
from jax.experimental import pallas as pl
from jax.experimental.pallas import tpu as pltpu
from jax.sharding import PartitionSpec as P

MODEL_WIDTH = 2048

CHUNKS = 4

epsilon = 1e-06
contract_last = (((1,), (1,)), ((), ()))
contract_first = (((0,), (0,)), ((), ()))
grid = ("pipe", "tensor")


def from_core(value):
    return lax.ppermute(value, "tensor", [(i, i ^ 1) for i in range(4)])


def to_rank(value, path):
    ranks = lax.axis_size("pipe")
    tensors = lax.axis_size("tensor")
    after = {p: path[(i + 1) % len(path)] for i, p in enumerate(path)}
    pairs = []
    for p in range(ranks):
        there = after.get(p, p if p ^ 1 in after else p ^ 1)
        for t in range(tensors):
            if there == p:
                other = t ^ 1
            elif p == path[-1] and len(path) > 2:
                other = t
            else:
                other = t % 2 * 2 + t // 2
            pairs.append((p * tensors + t, there * tensors + other))
    return lax.ppermute(value, grid, pairs)


def from_twin(value):
    ranks = lax.axis_size("pipe")
    tensors = lax.axis_size("tensor")
    pairs = [
        (p * tensors + t, (p ^ 1) * tensors + (t ^ 2))
        for p in range(ranks)
        for t in range(tensors)
    ]
    return lax.ppermute(value, grid, pairs)


def from_replica(value, by):
    groups = lax.axis_size("dp")
    return lax.ppermute(value, "dp", [(i, (i + by) % groups) for i in range(groups)])


def gelu_pair(value):
    root = jnp.float32(0.7978845608028654)
    square = value * value
    inner = root * (value + 0.044715 * square * value)
    bend = jnp.tanh(inner)
    half = 0.5 * (1.0 + bend)
    slope = half + 0.5 * value * (1.0 - bend * bend) * root * (1.0 + 3 * 0.044715 * square)
    return value * half, slope


def whole_rows(piece, core):
    across = from_twin(piece)
    upper = lax.axis_index("tensor") // 2
    first = jnp.where(upper == 0, piece, across)
    second = jnp.where(upper == 0, across, piece)
    mine = jnp.concatenate([first, second], axis=1)
    theirs = from_core(mine)
    low = jnp.where(core == 0, mine, theirs)
    high = jnp.where(core == 0, theirs, mine)
    share = piece.shape[1]
    return jnp.concatenate(
        [low[:, :share], high[:, :share], low[:, share:], high[:, share:]], axis=1
    )


def send(parts, paths):
    tokens = parts[0].shape[0]
    theirs = from_core(jnp.concatenate([part.astype(jnp.bfloat16) for part in parts], axis=0))
    come = []
    for i, (part, path) in enumerate(zip(parts, paths)):
        other = theirs[i * tokens : (i + 1) * tokens].astype(jnp.float32)
        come.append(to_rank((part + other).astype(jnp.bfloat16), path))
    return come


def settle(come):
    held = []
    for item in come:
        other = from_core(item).astype(jnp.float32)
        held.append((item.astype(jnp.float32) + other).astype(jnp.bfloat16))
    return held


def turn_block(from_ref, token_ref, to_ref):
    block = from_ref.shape[0]
    row = lax.broadcasted_iota(jnp.int32, (block, block), 0)
    column = lax.broadcasted_iota(jnp.int32, (block, block), 1)
    unit = jnp.where(row == column, 1.0, 0.0).astype(jnp.bfloat16)
    for first in range(0, from_ref.shape[1], block):
        to_ref[first : first + block, :] = lax.dot_general(
            unit,
            from_ref[:, first : first + block],
            contract_last,
            preferred_element_type=jnp.float32,
        ).astype(jnp.bfloat16)


def turned(weight, token, block):
    rows, columns = weight.shape
    return pl.pallas_call(
        turn_block,
        out_shape=jax.ShapeDtypeStruct((columns, rows), weight.dtype),
        grid=(rows // block,),
        in_specs=[
            pl.BlockSpec((block, columns), lambda i: (i, 0)),
            pl.BlockSpec(memory_space=pl.ANY),
        ],
        out_specs=pl.BlockSpec((columns, block), lambda i: (0, i)),
        compiler_params=pltpu.CompilerParams(vmem_limit_bytes=6 * 2**20),
        cost_estimate=pl.CostEstimate(
            flops=2 * rows * columns * block, bytes_accessed=4 * rows * columns, transcendentals=0
        ),
    )(weight, token)


def put(stack, item, index):
    return lax.dynamic_update_index_in_dim(stack, item, index, 0)


def take(stack, index):
    return lax.dynamic_index_in_dim(stack, index, 0, keepdims=False)


def terms(first, second, share):
    up_term = lax.dot_general(
        first[:, :share], second[:, share:], contract_first, preferred_element_type=jnp.float32
    )
    down_term = lax.dot_general(
        first[:, share:], second[:, :share], contract_first, preferred_element_type=jnp.float32
    )
    return up_term, down_term


def local(stream_a, stream_b, target_a, target_b, up_weight, down_weight):
    ranks = lax.axis_size("pipe")
    place = lax.axis_index("pipe")
    core = lax.axis_index("tensor") % 2
    groups = lax.axis_size("dp")
    member = lax.axis_index("dp")
    up = up_weight[0]
    down = down_weight[0]
    share = stream_a.shape[2]
    half = CHUNKS // 2
    hid = up.shape[1]
    flat = lambda value: value.reshape(-1, share)
    source = whole_rows(flat(stream_a), core).reshape(half, -1, MODEL_WIDTH)
    others = jnp.concatenate([flat(item) for item in (stream_b, target_a, target_b)], axis=0)
    others = whole_rows(others, core).reshape(3 * half, -1, MODEL_WIDTH)
    source = [source[i] for i in range(half)] + [others[i] for i in range(half)]
    target = [others[i] for i in range(half, 3 * half)]
    tokens = source[0].shape[0]
    stash = (
        jnp.zeros((CHUNKS + 1, tokens, 1), jnp.float32),
        jnp.zeros((CHUNKS + 1, tokens, MODEL_WIDTH), jnp.bfloat16),
        jnp.zeros((CHUNKS + 1, tokens, hid), jnp.bfloat16),
        jnp.zeros((CHUNKS + 1, tokens, hid), jnp.float32),
    )
    kept = (
        jnp.zeros((CHUNKS + 1, tokens, MODEL_WIDTH), jnp.bfloat16),
        jnp.zeros((CHUNKS + 1, tokens, hid), jnp.bfloat16),
    )
    steps = ranks + CHUNKS - 1
    come = []
    coming = {}
    arrived = {}
    early = slice(0, half)
    late = slice(half, CHUNKS)

    def cut(value, by):
        return lax.dynamic_slice_in_dim(value, ((member + by) % groups) * share, share, 1)

    def bundle(wide, narrow, which, by):
        wide = wide[which].reshape(-1, MODEL_WIDTH)
        narrow = narrow[which].reshape(-1, hid)
        return jnp.concatenate([cut(wide, by), narrow], axis=1)

    windows = {
        steps - 1: [("ahead", early, 1)],
        steps: [("ahead", early, 2)],
        steps + 1: [("ahead", early, 3), ("ahead", late, 1)],
        steps + 2: [("ahead", late, 2), ("ahead", late, 3)],
        steps + ranks - 4: [("behind", early, 1), ("behind", early, 3)],
        steps + ranks - 3: [("behind", early, 2)],
    }
    for step in range(steps + ranks - 1):
        turn = step - (ranks - 1)
        moving = step < steps
        held = []
        if step == 3:
            come[0], down_turned = lax.optimization_barrier((come[0], down_turned))
        if step == 4:
            come[0], up_turned = lax.optimization_barrier((come[0], up_turned))
        if coming:
            come, coming = lax.optimization_barrier((come, coming))
            arrived.update(coming)
            coming = {}
        if come:
            held = settle(come)
        parts = []
        ways = []
        if moving:
            if step == 0:
                now = source[0]
            else:
                now = held.pop(0)
                if step < CHUNKS:
                    now = jnp.where(place == 0, source[step], now)
            slot = jnp.clip(step - place, 0, CHUNKS)
            wide = now.astype(jnp.float32)
            scale = lax.rsqrt(jnp.mean(wide * wide, axis=1, keepdims=True) + epsilon)
            normed = (wide * scale).astype(jnp.bfloat16)
            if step == 2:
                down_turned = turned(down, now, 256)
            if step == 3:
                up_turned = turned(up, now, 256)
            hidden = jnp.dot(normed, up, preferred_element_type=jnp.float32)
            active, slope = gelu_pair(hidden)
            active = active.astype(jnp.bfloat16)
            items = (scale, normed, active, slope)
            stash = tuple(put(stack, item, slot) for stack, item in zip(stash, items))
            if step < steps - 1:
                part = jnp.dot(active, down, preferred_element_type=jnp.float32) + 0.25 * wide
                parts.append(part)
                ways.append(range(max(0, step - CHUNKS + 1), min(ranks, step + 2)))
        if turn >= 0:
            if turn == 0:
                now = target[0]
            else:
                now = held.pop(0)
                if turn < CHUNKS:
                    now = jnp.where(place == ranks - 1, target[turn], now)
            slot = jnp.clip(turn - (ranks - 1 - place), 0, CHUNKS)
            back = jnp.dot(now, down_turned, preferred_element_type=jnp.float32)
            scale, normed, active, slope = (take(stack, slot) for stack in stash)
            delta = (back * slope).astype(jnp.bfloat16)
            kept = tuple(put(stack, item, slot) for stack, item in zip(kept, (now, delta)))
            if turn < steps - 1:
                push = jnp.dot(delta, up_turned, preferred_element_type=jnp.float32)
                unit = normed.astype(jnp.float32)
                inner = jnp.sum(push * unit, axis=1, keepdims=True) / MODEL_WIDTH
                part = 0.25 * now.astype(jnp.float32) + scale * (push - unit * inner)
                parts.append(part)
                most = min(ranks - 1, ranks - 2 - turn + CHUNKS)
                ways.append(range(most, max(-1, ranks - 3 - turn), -1))
        if parts:
            come = send(parts, ways)
        for kind, which, by in windows.get(step, []):
            pair = (stash[1], stash[2]) if kind == "ahead" else kept
            name = kind + str(which.start) + str(by)
            coming[name] = from_replica(bundle(*pair, which, by), by)

    def gathered(kind, pair, which):
        pieces = [bundle(*pair, which, 0)]
        for by in range(1, groups):
            name = kind + str(which.start) + str(by)
            if name not in arrived:
                arrived[name] = from_replica(bundle(*pair, which, by), by)
            pieces.append(arrived[name])
        return pieces

    ahead = (stash[1], stash[2])
    first = gathered("ahead", ahead, early) + gathered("ahead", ahead, late)
    second = gathered("behind", kept, early) + gathered("behind", kept, late)
    first = jnp.concatenate(first, axis=0)
    second = jnp.concatenate(second, axis=0)
    up_sum, down_sum = terms(first, second, share)
    return (up_sum[None], down_sum[None])


def solution(mesh):
    return jax.shard_map(
        local,
        mesh=mesh,
        in_specs=(
            P("dp", None, "tensor"),
            P("dp", None, "tensor"),
            P("dp", None, "tensor"),
            P("dp", None, "tensor"),
            P("pipe", None, "tensor"),
            P("pipe", "tensor", None),
        ),
        out_specs=(P("pipe", "dp", "tensor"), P("pipe", "tensor", "dp")),
        check_vma=False,
    )
```

```python
import jax
import jax.numpy as jnp
from jax import lax
from jax.experimental import pallas as pl
from jax.experimental.pallas import tpu as pltpu
from jax.sharding import PartitionSpec as P

MODEL_WIDTH = 2048

CHUNKS = 4

epsilon = 1e-06
contract_last = (((1,), (1,)), ((), ()))
contract_first = (((0,), (0,)), ((), ()))
grid = ("pipe", "tensor")


def from_core(value):
    return lax.ppermute(value, "tensor", [(i, i ^ 1) for i in range(4)])


def to_rank(value, path):
    ranks = lax.axis_size("pipe")
    tensors = lax.axis_size("tensor")
    after = {p: path[(i + 1) % len(path)] for i, p in enumerate(path)}
    pairs = []
    for p in range(ranks):
        there = after.get(p, p if p ^ 1 in after else p ^ 1)
        for t in range(tensors):
            if there == p:
                other = t ^ 1
            elif p == path[-1] and len(path) > 2:
                other = t
            else:
                other = t % 2 * 2 + t // 2
            pairs.append((p * tensors + t, there * tensors + other))
    return lax.ppermute(value, grid, pairs)


def from_twin(value):
    ranks = lax.axis_size("pipe")
    tensors = lax.axis_size("tensor")
    pairs = [
        (p * tensors + t, (p ^ 1) * tensors + (t ^ 2))
        for p in range(ranks)
        for t in range(tensors)
    ]
    return lax.ppermute(value, grid, pairs)


def from_replica(value, by):
    groups = lax.axis_size("dp")
    return lax.ppermute(value, "dp", [(i, (i + by) % groups) for i in range(groups)])


def gelu_pair(value):
    root = jnp.float32(0.7978845608028654)
    square = value * value
    inner = root * (value + 0.044715 * square * value)
    bend = jnp.tanh(inner)
    half = 0.5 * (1.0 + bend)
    slope = half + 0.5 * value * (1.0 - bend * bend) * root * (1.0 + 3 * 0.044715 * square)
    return value * half, slope


def whole_rows(piece, core):
    across = from_twin(piece)
    upper = lax.axis_index("tensor") // 2
    first = jnp.where(upper == 0, piece, across)
    second = jnp.where(upper == 0, across, piece)
    mine = jnp.concatenate([first, second], axis=1)
    theirs = from_core(mine)
    low = jnp.where(core == 0, mine, theirs)
    high = jnp.where(core == 0, theirs, mine)
    share = piece.shape[1]
    return jnp.concatenate(
        [low[:, :share], high[:, :share], low[:, share:], high[:, share:]], axis=1
    )


def send(parts, paths):
    tokens = parts[0].shape[0]
    theirs = from_core(jnp.concatenate([part.astype(jnp.bfloat16) for part in parts], axis=0))
    come = []
    for i, (part, path) in enumerate(zip(parts, paths)):
        other = theirs[i * tokens : (i + 1) * tokens].astype(jnp.float32)
        come.append(to_rank((part + other).astype(jnp.bfloat16), path))
    return come


def settle(come):
    held = []
    for item in come:
        other = from_core(item).astype(jnp.float32)
        held.append((item.astype(jnp.float32) + other).astype(jnp.bfloat16))
    return held


def turn_block(from_ref, token_ref, to_ref):
    block = from_ref.shape[0]
    row = lax.broadcasted_iota(jnp.int32, (block, block), 0)
    column = lax.broadcasted_iota(jnp.int32, (block, block), 1)
    unit = jnp.where(row == column, 1.0, 0.0).astype(jnp.bfloat16)
    for first in range(0, from_ref.shape[1], block):
        to_ref[first : first + block, :] = lax.dot_general(
            unit,
            from_ref[:, first : first + block],
            contract_last,
            preferred_element_type=jnp.float32,
        ).astype(jnp.bfloat16)


def turned(weight, token, block):
    rows, columns = weight.shape
    return pl.pallas_call(
        turn_block,
        out_shape=jax.ShapeDtypeStruct((columns, rows), weight.dtype),
        grid=(rows // block,),
        in_specs=[
            pl.BlockSpec((block, columns), lambda i: (i, 0)),
            pl.BlockSpec(memory_space=pl.ANY),
        ],
        out_specs=pl.BlockSpec((columns, block), lambda i: (0, i)),
        compiler_params=pltpu.CompilerParams(vmem_limit_bytes=6 * 2**20),
        cost_estimate=pl.CostEstimate(
            flops=2 * rows * columns * block, bytes_accessed=4 * rows * columns, transcendentals=0
        ),
    )(weight, token)


def put(stack, item, index):
    return lax.dynamic_update_index_in_dim(stack, item, index, 0)


def take(stack, index):
    return lax.dynamic_index_in_dim(stack, index, 0, keepdims=False)


def terms(first, second, share):
    up_term = lax.dot_general(
        first[:, :share], second[:, share:], contract_first, preferred_element_type=jnp.float32
    )
    down_term = lax.dot_general(
        first[:, share:], second[:, :share], contract_first, preferred_element_type=jnp.float32
    )
    return up_term, down_term


def local(stream_a, stream_b, target_a, target_b, up_weight, down_weight):
    ranks = lax.axis_size("pipe")
    place = lax.axis_index("pipe")
    core = lax.axis_index("tensor") % 2
    groups = lax.axis_size("dp")
    member = lax.axis_index("dp")
    up = up_weight[0]
    down = down_weight[0]
    share = stream_a.shape[2]
    half = CHUNKS // 2
    hid = up.shape[1]
    flat = lambda value: value.reshape(-1, share)
    source = whole_rows(flat(stream_a), core).reshape(half, -1, MODEL_WIDTH)
    others = jnp.concatenate([flat(item) for item in (stream_b, target_a, target_b)], axis=0)
    others = whole_rows(others, core).reshape(3 * half, -1, MODEL_WIDTH)
    source = [source[i] for i in range(half)] + [others[i] for i in range(half)]
    target = [others[i] for i in range(half, 3 * half)]
    tokens = source[0].shape[0]
    stash = (
        jnp.zeros((CHUNKS + 1, tokens, 1), jnp.float32),
        jnp.zeros((CHUNKS + 1, tokens, MODEL_WIDTH), jnp.bfloat16),
        jnp.zeros((CHUNKS + 1, tokens, hid), jnp.bfloat16),
        jnp.zeros((CHUNKS + 1, tokens, hid), jnp.float32),
    )
    kept = (
        jnp.zeros((CHUNKS + 1, tokens, MODEL_WIDTH), jnp.bfloat16),
        jnp.zeros((CHUNKS + 1, tokens, hid), jnp.bfloat16),
    )
    steps = ranks + CHUNKS - 1
    come = []
    coming = {}
    arrived = {}
    early = slice(0, half)
    late = slice(half, CHUNKS)

    def cut(value, by):
        return lax.dynamic_slice_in_dim(value, ((member + by) % groups) * share, share, 1)

    def bundle(wide, narrow, which, by):
        wide = wide[which].reshape(-1, MODEL_WIDTH)
        narrow = narrow[which].reshape(-1, hid)
        return jnp.concatenate([cut(wide, by), narrow], axis=1)

    windows = {
        steps - 1: [("ahead", early, 1)],
        steps: [("ahead", early, 2)],
        steps + 1: [("ahead", early, 3), ("ahead", late, 1)],
        steps + 2: [("ahead", late, 2), ("ahead", late, 3)],
        steps + ranks - 4: [("behind", early, 1), ("behind", early, 3)],
        steps + ranks - 3: [("behind", early, 2)],
    }
    for step in range(steps + ranks - 1):
        turn = step - (ranks - 1)
        moving = step < steps
        held = []
        if step == 4:
            come[0], down_turned = lax.optimization_barrier((come[0], down_turned))
        if step == 5:
            come[0], up_turned = lax.optimization_barrier((come[0], up_turned))
        if coming:
            come, coming = lax.optimization_barrier((come, coming))
            arrived.update(coming)
            coming = {}
        if come:
            held = settle(come)
        parts = []
        ways = []
        if moving:
            if step == 0:
                now = source[0]
            else:
                now = held.pop(0)
                if step < CHUNKS:
                    now = jnp.where(place == 0, source[step], now)
            slot = jnp.clip(step - place, 0, CHUNKS)
            wide = now.astype(jnp.float32)
            scale = lax.rsqrt(jnp.mean(wide * wide, axis=1, keepdims=True) + epsilon)
            normed = (wide * scale).astype(jnp.bfloat16)
            if step == 3:
                down_turned = turned(down, now, 256)
            if step == 4:
                up_turned = turned(up, now, 256)
            hidden = jnp.dot(normed, up, preferred_element_type=jnp.float32)
            active, slope = gelu_pair(hidden)
            active = active.astype(jnp.bfloat16)
            items = (scale, normed, active, slope)
            stash = tuple(put(stack, item, slot) for stack, item in zip(stash, items))
            if step < steps - 1:
                part = jnp.dot(active, down, preferred_element_type=jnp.float32) + 0.25 * wide
                parts.append(part)
                ways.append(range(max(0, step - CHUNKS + 1), min(ranks, step + 2)))
        if turn >= 0:
            if turn == 0:
                now = target[0]
            else:
                now = held.pop(0)
                if turn < CHUNKS:
                    now = jnp.where(place == ranks - 1, target[turn], now)
            slot = jnp.clip(turn - (ranks - 1 - place), 0, CHUNKS)
            back = jnp.dot(now, down_turned, preferred_element_type=jnp.float32)
            scale, normed, active, slope = (take(stack, slot) for stack in stash)
            delta = (back * slope).astype(jnp.bfloat16)
            kept = tuple(put(stack, item, slot) for stack, item in zip(kept, (now, delta)))
            if turn < steps - 1:
                push = jnp.dot(delta, up_turned, preferred_element_type=jnp.float32)
                unit = normed.astype(jnp.float32)
                inner = jnp.sum(push * unit, axis=1, keepdims=True) / MODEL_WIDTH
                part = 0.25 * now.astype(jnp.float32) + scale * (push - unit * inner)
                parts.append(part)
                most = min(ranks - 1, ranks - 2 - turn + CHUNKS)
                ways.append(range(most, max(-1, ranks - 3 - turn), -1))
        if parts:
            come = send(parts, ways)
        for kind, which, by in windows.get(step, []):
            pair = (stash[1], stash[2]) if kind == "ahead" else kept
            name = kind + str(which.start) + str(by)
            coming[name] = from_replica(bundle(*pair, which, by), by)

    def gathered(kind, pair, which):
        pieces = [bundle(*pair, which, 0)]
        for by in range(1, groups):
            name = kind + str(which.start) + str(by)
            if name not in arrived:
                arrived[name] = from_replica(bundle(*pair, which, by), by)
            pieces.append(arrived[name])
        return pieces

    ahead = (stash[1], stash[2])
    first = gathered("ahead", ahead, early) + gathered("ahead", ahead, late)
    second = gathered("behind", kept, early) + gathered("behind", kept, late)
    first = jnp.concatenate(first, axis=0)
    second = jnp.concatenate(second, axis=0)
    up_sum, down_sum = terms(first, second, share)
    return (up_sum[None], down_sum[None])


def solution(mesh):
    return jax.shard_map(
        local,
        mesh=mesh,
        in_specs=(
            P("dp", None, "tensor"),
            P("dp", None, "tensor"),
            P("dp", None, "tensor"),
            P("dp", None, "tensor"),
            P("pipe", None, "tensor"),
            P("pipe", "tensor", None),
        ),
        out_specs=(P("pipe", "dp", "tensor"), P("pipe", "tensor", "dp")),
        check_vma=False,
    )
```
